256 devices in a mesh: cam: 8 (over x, y_lo), tm: 32 (over z, y_hi, core).
Axes of the slice: x: 4, y: 4 (y_hi: 2, y_lo: 2; y = y_hi * 2 + y_lo), z: 8, core: 2. Of those that a mesh axis runs over, the one named last changes fastest.
Arguments:
- queries: bfloat16 [8, 512, 8, 1536], P('cam', 'tm'), may hold values from -6 to 6
- keys: bfloat16 [8, 512, 8, 1536], P('cam', 'tm'), may hold values from -6 to 6
- values: bfloat16 [8, 512, 8, 1536], P('cam', 'tm'), may hold values from -6 to 6
- cam_valid: int32 [8, 512], P('cam', 'tm'), may hold values 0 or 1
- windows: int32 [12], replicated, may hold values from 1 to 64, as said below
- actions: int32 [512, 7], P('tm'), may hold values from 0 to 255
- act_table: bfloat16 [7, 256, 1536], replicated, may hold values from -1.796875 to 1.796875
- w_out: bfloat16 [1536, 1536], P('tm'), may hold values from -0.15625 to 0.15625
- cotangent: bfloat16 [8, 512, 8, 1536], P('cam', 'tm'), may hold values from -6 to 6
Outputs:
- predicted: bfloat16 [8, 512, 8, 1536], P('cam', 'tm')
- grad_queries: bfloat16 [8, 512, 8, 1536], P('cam', 'tm')
- grad_keys: bfloat16 [8, 512, 8, 1536], P('cam', 'tm')
- grad_values: bfloat16 [8, 512, 8, 1536], P('cam', 'tm')
- grad_out_weight: float32 [1536, 1536], P(('cam', 'tm'))
The draws below stay inside these ranges and needn't reach their ends.
Inputs may be any that keep to these rules, and one draw needn't show every extreme that they name: `windows`: some entry equals 64.
All inputs are finite; a program needn't handle non-finite values. No bound on the sum of `cam_valid` on one device may be relied on, other than what follows from the above.
Results may differ from the reference program's by a relative error of at most 0.009.
Values may be sent and summed in bfloat16 or wider, within the bound.
No kernel may reach another device: no remote copies, remote signals or barrier semaphores. Data moves between devices by JAX's collectives and lax.ppermute only.
A program may use at most 128 MiB of HBM per device.

```python
import jax
import jax.numpy as jnp
from jax import lax

D = 1536
HC = 12
HT = 12
HD = 64
ACT_DIMS = 7
BINS = 256
P_SIZE = 8
WIN = 64
CAMS = 8
NF = 512
NTOK = 32768


def drawn_pair(key):
    query_base = jax.random.normal(jax.random.fold_in(key, 21), (CAMS, NF, P_SIZE, D), jnp.float32)
    key_base = jax.random.normal(jax.random.fold_in(key, 22), (CAMS, NF, P_SIZE, D), jnp.float32)
    return (jnp.clip(query_base, -6.0, 6.0), jnp.clip(key_base, -6.0, 6.0))


def draw_queries(key, part):
    return drawn_pair(key)[0].astype(jnp.bfloat16)


def draw_keys(key, part):
    return drawn_pair(key)[1].astype(jnp.bfloat16)


def draw_windows(key, part):
    spans = jax.random.randint(jax.random.fold_in(key, 7), (HT,), 1, WIN + 1)
    widest = jax.random.randint(jax.random.fold_in(key, 8), (), 0, HT)
    return jnp.where(jnp.arange(HT) == widest, WIN, spans).astype(jnp.int32)


def place_ends(entries, rng, low, top_value):
    place = [jax.random.randint(jax.random.fold_in(rng, axis), (), 0, length) for axis, length in enumerate(entries.shape)]
    longest = entries.shape.index(max(entries.shape))
    next_to = place[:longest] + [(place[longest] + 1) % entries.shape[longest]] + place[longest + 1:]
    return entries.at[tuple(place)].set(low).at[tuple(next_to)].set(top_value)


def block_scale(own_key, shape, shards, low, high):
    def one(dim, blocks):
        draws = jax.random.uniform(jax.random.fold_in(jax.random.fold_in(own_key, 6), dim), (blocks,), jnp.float32, low / len(shards), high / len(shards))
        return jnp.repeat(jnp.exp(draws), shape[dim] // blocks).reshape((-1,) + (1,) * (len(shape) - dim - 1))

    loudness = one(*shards[0])
    for cut in shards[1:]:
        loudness = loudness * one(*cut)
    return loudness


def centred(own_key, dims, spread, limit, split=(), kind=jnp.bfloat16):
    result = spread * jax.random.normal(own_key, dims, jnp.float32)
    if split:
        result = result * block_scale(own_key, dims, split, -0.22, 0.18)
    return jnp.clip(result, -limit, limit).astype(kind)


def setup_inputs(seed: int = 0) -> dict:
    arg_keys = jax.random.split(jax.random.key(seed), 10)
    queries = draw_queries(jax.random.fold_in(arg_keys[9], 71), 0)
    keys = draw_keys(jax.random.fold_in(arg_keys[9], 71), 0)
    values = centred(arg_keys[2], (CAMS, NF, P_SIZE, D), 1.0, 6.0, ((0, 8), (1, 32)))
    cam_valid = place_ends((jax.random.randint(arg_keys[3], (CAMS, NF), 0, 4) < 3).astype(jnp.int32), jax.random.fold_in(arg_keys[3], 1), 0, 1)
    windows = draw_windows(jax.random.fold_in(arg_keys[9], 71), 0)
    actions = place_ends(jax.random.randint(arg_keys[5], (NF, ACT_DIMS), 0, BINS), jax.random.fold_in(arg_keys[5], 1), 0, BINS - 1).astype(jnp.int32)
    act_table = centred(arg_keys[6], (ACT_DIMS, BINS, D), 0.3, 1.796875)
    w_out = centred(arg_keys[7], (D, D), D ** -0.5, 0.15625, ((0, 32),))
    cotangent = centred(arg_keys[8], (CAMS, NF, P_SIZE, D), 1.0, 6.0, ((0, 8), (1, 32)))
    return dict(queries=queries, keys=keys, values=values, cam_valid=cam_valid, windows=windows, actions=actions, act_table=act_table, w_out=w_out, cotangent=cotangent)


def heads_of(tensor, first, count):
    segment = tensor[..., first * HD:(first + count) * HD]
    return segment.reshape(segment.shape[:-1] + (count, HD)).astype(jnp.float32)


def rounded(tensor):
    return lax.optimization_barrier(tensor.astype(jnp.bfloat16)).astype(jnp.float32)


def cross_frame(inputs):
    query_rows, key_rows, value_rows, valid_views, grad_rows = inputs
    score_scale = HD ** -0.5
    scores = jnp.einsum("cphd,erhd->chper", query_rows, key_rows) * score_scale
    camera_index = jnp.arange(CAMS)
    allowed = (valid_views[None, :] > 0) | (camera_index[:, None] == camera_index[None, :])
    scores = jnp.where(allowed[:, None, None, :, None], scores, -jnp.inf)
    largest = jnp.max(scores, axis=(3, 4), keepdims=True)
    exponent = jnp.exp(scores - largest)
    probability = exponent / jnp.sum(exponent, axis=(3, 4), keepdims=True)
    weights = rounded(probability)
    attended = jnp.einsum("chper,erhd->cphd", weights, value_rows)
    grad_weights = jnp.einsum("cphd,erhd->chper", grad_rows, value_rows)
    grad_scores = rounded(probability * (grad_weights - jnp.sum(probability * grad_weights, axis=(3, 4), keepdims=True)))
    grad_query = jnp.einsum("chper,erhd->cphd", grad_scores, key_rows) * score_scale
    grad_key = jnp.sum(rounded(jnp.einsum("chper,cphd->cerhd", grad_scores, query_rows) * score_scale), axis=0)
    grad_value = jnp.sum(rounded(jnp.einsum("chper,cphd->cerhd", weights, grad_rows)), axis=0)
    return attended, grad_query, grad_key, grad_value


def reference(queries, keys, values, cam_valid, windows, actions, act_table, w_out, cotangent):
    model_width = queries.shape[-1]
    cross_width = HC * HD
    grad_attn = jnp.dot(cotangent.reshape(-1, model_width), w_out.T, preferred_element_type=jnp.float32)
    grad_attn = grad_attn.astype(jnp.bfloat16).reshape(queries.shape)

    def frame_major(tensor, first, count):
        return jnp.moveaxis(heads_of(tensor, first, count), 1, 0)

    cross_out = lax.map(cross_frame, (frame_major(queries, 0, HC), frame_major(keys, 0, HC), frame_major(values, 0, HC), jnp.moveaxis(cam_valid, 1, 0), frame_major(grad_attn, 0, HC)))
    cross_attn, cross_dq, cross_dk, cross_dv = [jnp.moveaxis(item, 0, 1).reshape(CAMS, NF, P_SIZE, cross_width) for item in cross_out]

    def time_camera(inputs):
        query_rows, key_rows, value_rows, grad_rows = inputs
        score_scale = HD ** -0.5
        pad_front = ((WIN - 1, 0), (0, 0), (0, 0), (0, 0))
        key_pad = jnp.pad(key_rows, pad_front)
        value_pad = jnp.pad(value_rows, pad_front)
        frame_index = jnp.arange(NF, dtype=jnp.int32)
        offsets = jnp.arange(WIN, dtype=jnp.int32)

        def score_one(offset):
            start = (WIN - 1 - offset).astype(jnp.int32)
            past_key = lax.dynamic_slice_in_dim(key_pad, start, NF, 0)
            past_value = lax.dynamic_slice_in_dim(value_pad, start, NF, 0)
            return jnp.sum(query_rows * past_key, axis=-1) * score_scale, jnp.sum(grad_rows * past_value, axis=-1)

        scores, grad_weights = lax.map(score_one, offsets)
        usable = (offsets[:, None, None] < windows[None, None, :]) & (frame_index[None, :, None] >= offsets[:, None, None])
        scores = jnp.where(usable[:, :, None, :], scores, -jnp.inf)
        largest = jnp.max(scores, axis=0, keepdims=True)
        exponent = jnp.exp(scores - largest)
        probability = exponent / jnp.sum(exponent, axis=0, keepdims=True)
        weights = rounded(probability)
        grad_scores = rounded(probability * (grad_weights - jnp.sum(probability * grad_weights, axis=0, keepdims=True)))

        def accumulate(carry, offset):
            attended, grad_query, grad_key_pad, grad_value_pad = carry
            start = (WIN - 1 - offset).astype(jnp.int32)
            weight = lax.dynamic_index_in_dim(weights, offset, 0, keepdims=False)[..., None]
            score = lax.dynamic_index_in_dim(grad_scores, offset, 0, keepdims=False)[..., None]
            attended = attended + weight * lax.dynamic_slice_in_dim(value_pad, start, NF, 0)
            grad_query = grad_query + score * lax.dynamic_slice_in_dim(key_pad, start, NF, 0)
            key_part = lax.dynamic_slice_in_dim(grad_key_pad, start, NF, 0) + score * query_rows
            grad_key_pad = lax.dynamic_update_slice_in_dim(grad_key_pad, key_part, start, 0)
            value_part = lax.dynamic_slice_in_dim(grad_value_pad, start, NF, 0) + weight * grad_rows
            grad_value_pad = lax.dynamic_update_slice_in_dim(grad_value_pad, value_part, start, 0)
            return (attended, grad_query, grad_key_pad, grad_value_pad), None

        initial = (jnp.zeros_like(query_rows), jnp.zeros_like(query_rows), jnp.zeros_like(key_pad), jnp.zeros_like(value_pad))
        final, unused = lax.scan(accumulate, initial, offsets)
        attended, grad_query, grad_key_pad, grad_value_pad = final
        return attended, grad_query * score_scale, grad_key_pad[WIN - 1:] * score_scale, grad_value_pad[WIN - 1:]

    time_out = lax.map(time_camera, (heads_of(queries, HC, HT), heads_of(keys, HC, HT), heads_of(values, HC, HT), heads_of(grad_attn, HC, HT)))
    time_attn, time_dq, time_dk, time_dv = [item.reshape(CAMS, NF, P_SIZE, model_width - cross_width) for item in time_out]

    attn = jnp.concatenate([cross_attn, time_attn], axis=-1).astype(jnp.bfloat16)
    flat_attn = attn.reshape(-1, model_width)
    mixed = jnp.dot(flat_attn, w_out, preferred_element_type=jnp.float32).reshape(CAMS, NF, P_SIZE, model_width)
    action_sum = jnp.sum(act_table[jnp.arange(ACT_DIMS)[None, :], actions].astype(jnp.float32), axis=1)
    predicted = (mixed + action_sum[None, :, None, :]).astype(jnp.bfloat16)
    grad_out_weight = jnp.dot(flat_attn.T, cotangent.reshape(-1, model_width), preferred_element_type=jnp.float32) * (NTOK ** -0.5)
    grad_queries = jnp.concatenate([cross_dq, time_dq], axis=-1).astype(jnp.bfloat16)
    grad_keys = jnp.concatenate([cross_dk, time_dk], axis=-1).astype(jnp.bfloat16)
    grad_values = jnp.concatenate([cross_dv, time_dv], axis=-1).astype(jnp.bfloat16)
    return (predicted, grad_queries, grad_keys, grad_values, grad_out_weight)
```

```python
import math

import jax
import jax.numpy as jnp
from jax import lax
from jax.experimental import pallas as pl
from jax.experimental.pallas import tpu as pltpu
from jax.sharding import PartitionSpec as P

HC = 12
HT = 12
HD = 64
WIN = 64
CW = HC * HD
GROUP = 4
SCALE = HD ** (-0.5)
BF = jnp.bfloat16
F32 = jnp.float32
PAIRS = HC // 2
VM = pl.BlockSpec(memory_space=pltpu.VMEM)
SM = pl.BlockSpec(memory_space=pltpu.SMEM)


def params():
    return pltpu.CompilerParams(vmem_limit_bytes=48 * 1024 * 1024)


def iota(shape, dim):
    return lax.broadcasted_iota(jnp.int32, shape, dim)


def dot_nt(a, b):
    return lax.dot_general(a, b, (((1,), (1,)), ((), ())), preferred_element_type=F32)


def dot_tn(a, b):
    return lax.dot_general(a, b, (((0,), (0,)), ((), ())), preferred_element_type=F32)


def dot_nn(a, b):
    return jnp.dot(a, b, preferred_element_type=F32)


def split_pair(rows):
    low = iota(rows.shape, 1) < HD
    zero = jnp.zeros_like(rows)
    return jnp.concatenate([jnp.where(low, rows, zero), jnp.where(low, zero, rows)], axis=0)


def join_pair(rows):
    count = rows.shape[0] // 2
    low = iota((count, rows.shape[1]), 1) < HD
    return jnp.where(low, rows[:count], rows[count:])


def softmax_pair(q, k, mask):
    scores = dot_nt(split_pair(q), k) * SCALE
    scores = jnp.where(mask, scores, -jnp.inf)
    largest = jnp.max(scores, axis=1, keepdims=True)
    e = jnp.exp(scores - largest)
    return e / jnp.sum(e, axis=1, keepdims=True)


def pack_kernel(valid, q, k, v, ct, view_ref, time_ref):
    rows = q.shape[0]
    per_cam = rows // 16
    row = iota((rows, rows), 0)
    col = iota((rows, rows), 1)
    frames = rows // 8
    source = ((row // 2) % frames) * 8 + 2 * (row // (2 * frames)) + row % 2
    perm = jnp.where(col == source, 1.0, 0.0).astype(BF)
    for i, ref in enumerate((q, k, v)):
        view_ref[:, i * CW : (i + 1) * CW] = ref[:, :CW]
        time_ref[:, i * CW : (i + 1) * CW] = dot_nn(perm, ref[:, CW:]).astype(BF)
    view_ref[:, 3 * CW : 5 * CW] = ct[...]
    time_ref[:, 3 * CW : 5 * CW] = dot_nn(perm, ct[...]).astype(BF)
    frame = iota((rows, 128), 0) // 8
    flags = jnp.zeros((rows, 128), F32)
    for f in range(frames):
        flags = jnp.where(frame == f, valid[0, f].astype(F32), flags)
    view_ref[:, 5 * CW :] = jnp.where(flags > 0.5, 1.0, 0.0).astype(BF)


def view_mask(flags):
    rows = flags.shape[0]
    pick = jnp.where(iota((8, 128), 1) == 0, 1.0, 0.0).astype(BF)
    valid_row = dot_nt(pick, flags)[:1]
    r = iota((2 * rows, rows), 0) % rows
    c = iota((2 * rows, rows), 1)
    same_frame = ((r // 8) % 2) == ((c // 8) % 2)
    return same_frame & ((valid_row > 0.5) | (r // 16 == c // 16))


def view_forward_kernel(x, attn_ref, prob_ref):
    mask = view_mask(x[:, 5 * CW :])
    for j in range(PAIRS):
        lanes = slice(128 * j, 128 * (j + 1))
        q = x[:, 128 * j : 128 * (j + 1)]
        k = x[:, CW + 128 * j : CW + 128 * (j + 1)]
        v = x[:, 2 * CW + 128 * j : 2 * CW + 128 * (j + 1)]
        prob = softmax_pair(q, k, mask)
        prob_ref[j] = prob
        attn_ref[:, lanes] = join_pair(dot_nn(prob.astype(BF), v)).astype(BF)


def time_forward_kernel(windows, block, x, prev, attn_ref, prob_ref):
    rows = x.shape[0]
    r = iota((2 * rows, 2 * rows), 0)
    c = iota((2 * rows, 2 * rows), 1)
    second = r >= rows
    r = r % rows
    key_frame = c // 2 - rows // 2
    gap = r // 2 - key_frame
    base = (r % 2 == c % 2) & (gap >= 0) & ((key_frame >= 0) | (block[0] > 0))
    for j in range(PAIRS):
        lanes = slice(128 * j, 128 * (j + 1))
        q = x[:, 128 * j : 128 * (j + 1)]
        k = jnp.concatenate([prev[:, lanes], x[:, CW + 128 * j : CW + 128 * (j + 1)]], axis=0)
        v = jnp.concatenate(
            [prev[:, CW + 128 * j : CW + 128 * (j + 1)], x[:, 2 * CW + 128 * j : 2 * CW + 128 * (j + 1)]],
            axis=0,
        )
        limit = jnp.where(second, windows[2 * j + 1], windows[2 * j])
        prob = softmax_pair(q, k, base & (gap < limit))
        prob_ref[j] = prob
        attn_ref[:, lanes] = join_pair(dot_nn(prob.astype(BF), v)).astype(BF)


def backward_pair(q, k, v, g, prob):
    g2 = split_pair(g)
    grad_prob = dot_nt(g2, v)
    total = jnp.sum(prob * grad_prob, axis=1, keepdims=True)
    grad_scores = (prob * (grad_prob - total)).astype(BF)
    dq = join_pair(dot_nn(grad_scores, k)) * SCALE
    dk = dot_tn(grad_scores, split_pair(q)) * SCALE
    dv = dot_tn(prob.astype(BF), g2)
    return dq, dk, dv


def view_backward_kernel(x, attn, prob_ref, w, out_ref):
    grad = dot_nt(x[:, 3 * CW : 5 * CW], w[...]).astype(BF)
    out_ref[:, :CW] = attn[...]
    for j in range(PAIRS):
        at = [slice(i * CW + 128 * j, i * CW + 128 * (j + 1)) for i in range(4)]
        dq, dk, dv = backward_pair(x[:, at[0]], x[:, at[1]], x[:, at[2]], grad[:, at[0]], prob_ref[j])
        out_ref[:, at[1]] = dq.astype(BF)
        out_ref[:, at[2]] = dk.astype(BF)
        out_ref[:, at[3]] = dv.astype(BF)


def time_backward_kernel(x, prev, prob_ref, w, dq_ref, own_ref, back_ref):
    rows = x.shape[0]
    grad = dot_nt(x[:, 3 * CW : 5 * CW], w[...]).astype(BF)
    for j in range(PAIRS):
        at = [slice(i * CW + 128 * j, i * CW + 128 * (j + 1)) for i in range(3)]
        k = jnp.concatenate([prev[:, at[0]], x[:, at[1]]], axis=0)
        v = jnp.concatenate([prev[:, at[1]], x[:, at[2]]], axis=0)
        dq, dk, dv = backward_pair(x[:, at[0]], k, v, grad[:, at[0]], prob_ref[j])
        dq_ref[:, at[0]] = dq.astype(BF)
        back_ref[:, at[0]] = dk[:rows].astype(BF)
        own_ref[:, at[0]] = dk[rows:]
        back_ref[:, at[1]] = dv[:rows].astype(BF)
        own_ref[:, at[1]] = dv[rows:]


def time_sum_kernel(attn, dq, own, back, out_ref):
    out_ref[:, :CW] = attn[...]
    out_ref[:, CW : 2 * CW] = dq[...]
    out_ref[:, 2 * CW :] = (own[...] + back[...].astype(F32)).astype(BF)


def finish_kernel(view, time, w, action, pred_ref, dq_ref, dk_ref, dv_ref):
    rows = view.shape[0]
    row = iota((rows, rows), 0)
    col = iota((rows, rows), 1)
    frames = rows // 8
    source = ((row // 2) % GROUP) * 2 * frames + (row // 8) * 2 + row % 2
    perm = jnp.where(col == source, 1.0, 0.0).astype(BF)
    for i, ref in enumerate((dq_ref, dk_ref, dv_ref), 1):
        part = slice(i * CW, (i + 1) * CW)
        ref[:, :CW] = view[:, part]
        ref[:, CW:] = dot_nn(perm, time[:, part]).astype(BF)
    attn_time = dot_nn(perm, time[:, :CW]).astype(BF)
    mixed = dot_nn(view[:, :CW], w[:CW]) + dot_nn(attn_time, w[CW:])
    total = mixed.reshape(frames, 8, 2 * CW) + action[...][:, None, :]
    pred_ref[...] = total.reshape(rows, 2 * CW).astype(BF)


def call(kernel, outs, specs, *args):
    return pl.pallas_call(
        kernel,
        out_shape=[jax.ShapeDtypeStruct(shape, kind) for shape, kind in outs],
        in_specs=specs,
        out_specs=[VM] * len(outs),
        compiler_params=params(),
    )(*args)


def shards(queries, keys, values, cam_valid, windows, actions, act_table, w_out, cotangent):
    _, frames, tokens, width = queries.shape
    rows = frames * tokens
    cams = lax.axis_size("cam")
    tm = lax.axis_size("tm")
    at_tm = lax.axis_index("tm")
    core = at_tm % 2
    fours = [[GROUP * i + j for j in range(GROUP)] for i in range(tm // GROUP)]
    same_core = [[2 * i + j for i in range(tm // 2)] for j in range(2)]
    swap = [(i, i ^ 1) for i in range(tm)]

    w_full = lax.all_gather(w_out, "tm", axis=0, tiled=True)
    q, k, v, ct = (a.reshape(rows, width) for a in (queries, keys, values, cotangent))
    view_send, time_send = call(
        pack_kernel,
        [((rows, 5 * CW + 128), BF), ((rows, 5 * CW), BF)],
        [SM] + [VM] * 4,
        cam_valid, q, k, v, ct,
    )
    view_x = lax.all_to_all(view_send, "cam", 0, 0, tiled=True)
    time_x = lax.all_to_all(time_send, "tm", 0, 0, tiled=True, axis_index_groups=fours)
    prev = lax.ppermute(
        time_x[:, CW : 3 * CW], "tm", [(i, i + GROUP) for i in range(tm - GROUP)]
    )

    attn_view, prob_view = call(
        view_forward_kernel, [((rows, CW), BF), ((PAIRS, 2 * rows, rows), F32)], [VM], view_x
    )
    attn_time, prob_time = call(
        time_forward_kernel,
        [((rows, CW), BF), ((PAIRS, 2 * rows, 2 * rows), F32)],
        [SM, SM, VM, VM],
        windows, (at_tm // GROUP).reshape(1), time_x, prev,
    )

    def half(which):
        return jnp.concatenate(
            [lax.dynamic_slice_in_dim(a[:, 3 * CW : 5 * CW], which * CW, CW, 1) for a in (view_x, time_x)],
            axis=1,
        )

    other_ct = lax.ppermute(half(1 - core), "tm", swap)
    own_ct = half(core)
    attn_both = jnp.concatenate([attn_view, attn_time], axis=1)
    other_attn = lax.ppermute(attn_both, "tm", swap)
    grad_norm = 1.0 / math.sqrt(cams * tm * rows)
    left = jnp.concatenate([attn_both, other_attn], axis=0)
    right = jnp.concatenate([own_ct, other_ct], axis=0)
    part = jnp.concatenate(
        [dot_tn(left[:, :CW], right[:, :CW]), dot_tn(left[:, CW:], right[:, CW:])], axis=0
    )
    part = (part * grad_norm).astype(BF)
    part = lax.all_to_all(part.reshape(cams, width // cams, CW), "cam", 0, 0, tiled=True)
    part = jnp.sum(part.astype(F32), axis=0).astype(BF)
    chips = tm // 2
    part = lax.all_to_all(
        part.reshape(chips, width // cams // chips, CW), "tm", 0, 0, tiled=True, axis_index_groups=same_core
    )
    part = jnp.sum(part.astype(F32), axis=0)
    final = width // cams // tm
    mine = lax.dynamic_slice_in_dim(part, core * final, final, 0)
    theirs = lax.ppermute(lax.dynamic_slice_in_dim(part, (1 - core) * final, final, 0), "tm", swap)
    grad_out_weight = jnp.concatenate(
        [jnp.where(core == 0, mine, theirs), jnp.where(core == 0, theirs, mine)], axis=1
    )

    codes = jnp.arange(act_table.shape[1])
    one_hot = (actions[:, :, None] == codes[None, None, :]).astype(BF).reshape(frames, -1)
    action_sum = jnp.dot(one_hot, act_table.reshape(-1, width), preferred_element_type=F32)

    (view_back,) = call(
        view_backward_kernel, [((rows, 4 * CW), BF)], [VM] * 4, view_x, attn_view, prob_view, w_full[:CW]
    )
    dq_time, own, back = call(
        time_backward_kernel,
        [((rows, CW), BF), ((rows, 2 * CW), F32), ((rows, 2 * CW), BF)],
        [VM] * 4,
        time_x, prev, prob_time, w_full[CW:],
    )
    returned = lax.ppermute(back, "tm", [(i + GROUP, i) for i in range(tm - GROUP)])
    view_back = lax.all_to_all(view_back, "cam", 0, 0, tiled=True)
    (time_back,) = call(time_sum_kernel, [((rows, 4 * CW), BF)], [VM] * 4, attn_time, dq_time, own, returned)
    time_back = lax.all_to_all(time_back, "tm", 0, 0, tiled=True, axis_index_groups=fours)
    outs = call(
        finish_kernel, [((rows, width), BF)] * 4, [VM] * 4, view_back, time_back, w_full, action_sum
    )
    return tuple(a.reshape(1, frames, tokens, width) for a in outs) + (grad_out_weight,)


def solution(mesh):
    in_specs = (
        P("cam", "tm", None, None),
        P("cam", "tm", None, None),
        P("cam", "tm", None, None),
        P("cam", "tm"),
        P(),
        P("tm", None),
        P(),
        P("tm", None),
        P("cam", "tm", None, None),
    )
    out_specs = (
        P("cam", "tm", None, None),
        P("cam", "tm", None, None),
        P("cam", "tm", None, None),
        P("cam", "tm", None, None),
        P(("cam", "tm"), None),
    )
    return jax.shard_map(shards, mesh=mesh, in_specs=in_specs, out_specs=out_specs, check_vma=False)
```

```python
import functools
import math

import jax
import jax.numpy as jnp
from jax import lax
from jax.experimental import pallas as pl
from jax.experimental.pallas import tpu as pltpu
from jax.sharding import PartitionSpec as P

HC = 12
HT = 12
HD = 64
WIN = 64
CW = HC * HD
GROUP = 4
SCALE = HD ** (-0.5)
BF = jnp.bfloat16
F32 = jnp.float32
PAIRS = HC // 2
VM = pl.BlockSpec(memory_space=pltpu.VMEM)
ANY = pl.BlockSpec(memory_space=pl.ANY)
SM = pl.BlockSpec(memory_space=pltpu.SMEM)


def params():
    return pltpu.CompilerParams(vmem_limit_bytes=56 * 1024 * 1024)


def iota(shape, dim):
    return lax.broadcasted_iota(jnp.int32, shape, dim)


def dot_nt(a, b):
    return lax.dot_general(a, b, (((1,), (1,)), ((), ())), preferred_element_type=F32)


def dot_tn(a, b):
    return lax.dot_general(a, b, (((0,), (0,)), ((), ())), preferred_element_type=F32)


def dot_nn(a, b):
    return jnp.dot(a, b, preferred_element_type=F32)


def split_pair(rows):
    low = iota(rows.shape, 1) < HD
    zero = jnp.zeros_like(rows)
    return jnp.concatenate([jnp.where(low, rows, zero), jnp.where(low, zero, rows)], axis=0)


def join_pair(rows):
    count = rows.shape[0] // 2
    low = iota((count, rows.shape[1]), 1) < HD
    return jnp.where(low, rows[:count], rows[count:])


def softmax_pair(q, k, mask):
    scores = dot_nt(split_pair(q), k) * SCALE
    scores = jnp.where(mask, scores, -jnp.inf)
    largest = jnp.max(scores, axis=1, keepdims=True)
    e = jnp.exp(scores - largest)
    return e / jnp.sum(e, axis=1, keepdims=True)


def pack_kernel(me, valid, q, k, v, ct, view_ref, *rest):
    own_refs, kv_refs, (held, sems) = rest[:GROUP], rest[GROUP : 2 * GROUP], rest[2 * GROUP :]
    copies = [pltpu.make_async_copy(ref, held.at[i], sems.at[i]) for i, ref in enumerate((q, k, v, ct))]
    for copy in copies:
        copy.start()
    rows = q.shape[0]
    frames = rows // 8
    block = 2 * frames
    row = iota((rows, rows), 0)
    col = iota((rows, rows), 1)
    member = (row // block) ^ me[0]
    source = ((row // 2) % frames) * 8 + 2 * member + row % 2
    perm = jnp.where(col == source, 1.0, 0.0).astype(BF)
    frame = iota((rows, 128), 0) // 8
    flags = jnp.zeros((rows, 128), F32)
    for f in range(frames):
        flags = jnp.where(frame == f, valid[0, f].astype(F32), flags)
    view_ref[:, 5 * CW :] = jnp.where(flags > 0.5, 1.0, 0.0).astype(BF)
    for i in range(4):
        copies[i].wait()
        if i < 3:
            part = slice(i * CW, (i + 1) * CW)
            view_ref[:, part] = held[i, :, :CW]
            moved = dot_nn(perm, held[i, :, CW:]).astype(BF)
        else:
            part = slice(3 * CW, 5 * CW)
            view_ref[:, part] = held[i]
            moved = dot_nn(perm, held[i]).astype(BF)
        for d in range(GROUP):
            own_refs[d][:, part] = moved[d * block : (d + 1) * block]
            if i in (1, 2):
                kv_refs[d][:, (i - 1) * CW : i * CW] = moved[d * block : (d + 1) * block]


def view_mask(flags):
    rows = flags.shape[0]
    pick = jnp.where(iota((8, 128), 1) == 0, 1.0, 0.0).astype(BF)
    valid_row = dot_nt(pick, flags)[:1]
    r = iota((2 * rows, rows), 0) % rows
    c = iota((2 * rows, rows), 1)
    same_frame = ((r // 8) % 2) == ((c // 8) % 2)
    return same_frame & ((valid_row > 0.5) | (r // 16 == c // 16))


def keep_for_weight(attn, ct, core, own_ref, send_ref):
    own_ref[:, :CW] = attn
    send_ref[:, :CW] = attn
    own_ref[:, CW:] = jnp.where(core == 0, ct[:, :CW], ct[:, CW:])
    send_ref[:, CW:] = jnp.where(core == 0, ct[:, CW:], ct[:, :CW])


def view_forward_kernel(me, x, own_ref, send_ref, prob_ref):
    mask = view_mask(x[:, 5 * CW :])
    attn = []
    for j in range(PAIRS):
        q = x[:, 128 * j : 128 * (j + 1)]
        k = x[:, CW + 128 * j : CW + 128 * (j + 1)]
        v = x[:, 2 * CW + 128 * j : 2 * CW + 128 * (j + 1)]
        prob = softmax_pair(q, k, mask)
        prob_ref[j] = prob
        attn.append(join_pair(dot_nn(prob.astype(BF), v)).astype(BF))
    keep_for_weight(jnp.concatenate(attn, axis=1), x[:, 3 * CW : 5 * CW], me[0] % 2, own_ref, send_ref)


def rows_of(refs, columns):
    return jnp.concatenate([ref[:, columns] for ref in refs], axis=0)


def time_forward_kernel(windows, me, block, *refs):
    x, prev, (own_ref, send_ref, prob_ref) = refs[:GROUP], refs[GROUP : 2 * GROUP], refs[2 * GROUP :]
    size = x[0].shape[0]
    rows = GROUP * size
    r = iota((2 * rows, 2 * rows), 0)
    c = iota((2 * rows, 2 * rows), 1)
    second = r >= rows

    def frame_of(row):
        return ((row // size) ^ me[0]) * (size // 2) + (row % size) // 2

    key_frame = frame_of(c % rows) - jnp.where(c < rows, rows // 2, 0)
    gap = frame_of(r % rows) - key_frame
    base = (r % 2 == c % 2) & (gap >= 0) & ((key_frame >= 0) | (block[0] > 0))
    attn = []
    for j in range(PAIRS):
        at = [slice(i * CW + 128 * j, i * CW + 128 * (j + 1)) for i in range(3)]
        k = jnp.concatenate([rows_of(prev, at[0]), rows_of(x, at[1])], axis=0)
        v = jnp.concatenate([rows_of(prev, at[1]), rows_of(x, at[2])], axis=0)
        limit = jnp.where(second, windows[2 * j + 1], windows[2 * j])
        prob = softmax_pair(rows_of(x, at[0]), k, base & (gap < limit))
        prob_ref[j] = prob
        attn.append(join_pair(dot_nn(prob.astype(BF), v)).astype(BF))
    keep_for_weight(
        jnp.concatenate(attn, axis=1), rows_of(x, slice(3 * CW, 5 * CW)), me[0] % 2, own_ref, send_ref
    )


def weight_kernel(scale, own_view, other_view, own_time, other_time, out_ref):
    for i, (own, other) in enumerate(((own_view, other_view), (own_time, other_time))):
        left = jnp.concatenate([own[:, :CW], other[:, :CW]], axis=0)
        right = jnp.concatenate([own[:, CW:], other[:, CW:]], axis=0)
        out_ref[i * CW : (i + 1) * CW, :] = (dot_tn(left, right) * scale).astype(BF)


def fetch_weight(me, own, other, held, sem, first, count):
    size = held.shape[0] // count
    core = me[0] % 2
    copies = []
    for i in range(count // 2):
        for which_at, (which, ref) in enumerate(((core, own), (1 - core, other))):
            start = pl.multiple_of((2 * i + which) * size, 16)
            copies.append(
                pltpu.make_async_copy(
                    ref.at[pl.ds((first // 2 + i) * size, size)], held.at[pl.ds(start, size)], sem.at[2 * i + which_at]
                )
            )
    for copy in copies:
        copy.start()
    return copies


def backward_pair(q, k, v, g, prob):
    g2 = split_pair(g)
    grad_prob = dot_nt(g2, v)
    total = jnp.sum(prob * grad_prob, axis=1, keepdims=True)
    grad_scores = (prob * (grad_prob - total)).astype(BF)
    dq = join_pair(dot_nn(grad_scores, k)) * SCALE
    dk = dot_tn(grad_scores, split_pair(q)) * SCALE
    dv = dot_tn(prob.astype(BF), g2)
    return dq, dk, dv


def view_backward_kernel(blocks, me, x, kept, prob_ref, w_own, w_other, out_ref, w, sem):
    copies = fetch_weight(me, w_own, w_other, w, sem, 0, blocks // 2)
    out_ref[:, :CW] = kept[:, :CW]
    for copy in copies:
        copy.wait()
    grad = dot_nt(x[:, 3 * CW : 5 * CW], w[...]).astype(BF)
    for j in range(PAIRS):
        at = [slice(i * CW + 128 * j, i * CW + 128 * (j + 1)) for i in range(4)]
        dq, dk, dv = backward_pair(x[:, at[0]], x[:, at[1]], x[:, at[2]], grad[:, at[0]], prob_ref[j])
        out_ref[:, at[1]] = dq.astype(BF)
        out_ref[:, at[2]] = dk.astype(BF)
        out_ref[:, at[3]] = dv.astype(BF)


def time_backward_kernel(blocks, me, *refs):
    x, prev = refs[:GROUP], refs[GROUP : 2 * GROUP]
    kept, prob_ref, w_own, w_other = refs[2 * GROUP : 2 * GROUP + 4]
    out_refs = refs[2 * GROUP + 4 : 3 * GROUP + 4]
    back_refs = refs[3 * GROUP + 4 : 4 * GROUP + 4]
    w, sem = refs[4 * GROUP + 4 :]
    copies = fetch_weight(me, w_own, w_other, w, sem, blocks // 2, blocks // 2)
    size = x[0].shape[0]
    rows = GROUP * size

    def store(out, columns, value):
        value = value.astype(BF)
        for d in range(GROUP):
            out[d][:, columns] = value[d * size : (d + 1) * size]

    store(out_refs, slice(0, CW), kept[:, :CW])
    for copy in copies:
        copy.wait()
    grad = dot_nt(rows_of(x, slice(3 * CW, 5 * CW)), w[...]).astype(BF)
    for j in range(PAIRS):
        at = [slice(i * CW + 128 * j, i * CW + 128 * (j + 1)) for i in range(4)]
        k = jnp.concatenate([rows_of(prev, at[0]), rows_of(x, at[1])], axis=0)
        v = jnp.concatenate([rows_of(prev, at[1]), rows_of(x, at[2])], axis=0)
        dq, dk, dv = backward_pair(rows_of(x, at[0]), k, v, grad[:, at[0]], prob_ref[j])
        store(out_refs, at[1], dq)
        store(back_refs, at[0], dk[:rows])
        store(out_refs, at[2], dk[rows:])
        store(back_refs, at[1], dv[:rows])
        store(out_refs, at[3], dv[rows:])


def finish_kernel(blocks, me, view, w_own, w_other, action, *refs):
    time, back = refs[:GROUP], refs[GROUP : 2 * GROUP]
    pred_ref, dq_ref, dk_ref, dv_ref, w, sem = refs[2 * GROUP :]
    copies = fetch_weight(me, w_own, w_other, w, sem, 0, blocks)
    rows = view.shape[0]
    frames = rows // 8
    row = iota((rows, rows), 0)
    col = iota((rows, rows), 1)
    source = (((row // 2) % GROUP) ^ me[0]) * 2 * frames + (row // 8) * 2 + row % 2
    perm = jnp.where(col == source, 1.0, 0.0).astype(BF)
    for i, ref in enumerate((dq_ref, dk_ref, dv_ref), 1):
        part = slice(i * CW, (i + 1) * CW)
        rows_time = rows_of(time, part)
        if i > 1:
            returned = rows_of(back, slice((i - 2) * CW, (i - 1) * CW))
            rows_time = (rows_time.astype(F32) + returned.astype(F32)).astype(BF)
        ref[:, :CW] = view[:, part]
        ref[:, CW:] = dot_nn(perm, rows_time).astype(BF)
    attn_time = dot_nn(perm, rows_of(time, slice(0, CW))).astype(BF)
    for copy in copies:
        copy.wait()
    mixed = dot_nn(view[:, :CW], w[:CW]) + dot_nn(attn_time, w[CW:])
    total = mixed.reshape(frames, 8, 2 * CW) + action[...][:, None, :]
    pred_ref[...] = total.reshape(rows, 2 * CW).astype(BF)


def whole(shape):
    return pl.BlockSpec(shape, lambda *at: (0,) * len(shape))


def call(kernel, outs, specs, *args, scratch=()):
    specs = [whole(arg.shape) if spec is VM else spec for spec, arg in zip(specs, args)]
    return pl.pallas_call(
        kernel,
        out_shape=[jax.ShapeDtypeStruct(shape, kind) for shape, kind in outs],
        in_specs=specs,
        out_specs=[whole(shape) for shape, _ in outs],
        grid=(1,),
        scratch_shapes=list(scratch),
        compiler_params=params(),
    )(*args)


def shards(queries, keys, values, cam_valid, windows, actions, act_table, w_out, cotangent):
    _, frames, tokens, width = queries.shape
    rows = frames * tokens
    block = rows // GROUP
    cams = lax.axis_size("cam")
    tm = lax.axis_size("tm")
    at_tm = lax.axis_index("tm")
    core = at_tm % 2
    me = (at_tm % GROUP).reshape(1)
    group = (at_tm // GROUP).reshape(1)
    same_core = [[2 * i + j for i in range(tm // 2)] for j in range(2)]
    swap = [(i, i ^ 1) for i in range(tm)]
    onward = [[(i, (i + GROUP) ^ d) for i in range(tm - GROUP)] for d in range(GROUP)]
    inward = [[((i + GROUP) ^ d, i) for i in range(tm - GROUP)] for d in range(GROUP)]
    within = [[(i, i ^ d) for i in range(tm)] for d in range(GROUP)]

    w_own = lax.all_gather(w_out, "tm", axis=0, tiled=True, axis_index_groups=same_core)
    w_other = lax.ppermute(w_own, "tm", swap)
    q, k, v, ct = (a.reshape(rows, width) for a in (queries, keys, values, cotangent))
    packed = call(
        pack_kernel,
        [((rows, 5 * CW + 128), BF)] + [((block, 5 * CW), BF)] * GROUP + [((block, 2 * CW), BF)] * GROUP,
        [SM, SM] + [ANY] * 4,
        me, cam_valid, q, k, v, ct,
        scratch=[pltpu.VMEM((4, rows, width), BF), pltpu.SemaphoreType.DMA((4,))],
    )
    view_send, time_send, kv_send = packed[0], packed[1 : GROUP + 1], packed[GROUP + 1 :]
    view_x = lax.all_to_all(view_send, "cam", 0, 0, tiled=True)
    time_x = [time_send[0]] + [lax.ppermute(time_send[d], "tm", within[d]) for d in range(1, GROUP)]
    prev = [lax.ppermute(kv_send[d], "tm", onward[d]) for d in range(GROUP)]

    kept_view, view_swap, prob_view = call(
        view_forward_kernel,
        [((rows, 2 * CW), BF)] * 2 + [((PAIRS, 2 * rows, rows), F32)],
        [SM, VM],
        me, view_x,
    )
    kept_time, time_swap, prob_time = call(
        time_forward_kernel,
        [((rows, 2 * CW), BF)] * 2 + [((PAIRS, 2 * rows, 2 * rows), F32)],
        [SM] * 3 + [VM] * (2 * GROUP),
        windows, me, group, *time_x, *prev,
    )

    view_swap = lax.ppermute(view_swap, "tm", swap)
    time_swap = lax.ppermute(time_swap, "tm", swap)
    grad_norm = 1.0 / math.sqrt(cams * tm * rows)
    (part,) = call(
        functools.partial(weight_kernel, grad_norm),
        [((width, CW), BF)],
        [VM] * 4,
        kept_view, view_swap, kept_time, time_swap,
    )
    part = lax.all_to_all(part.reshape(cams, width // cams, CW), "cam", 0, 0, tiled=True)
    part = jnp.sum(part.astype(F32), axis=0).astype(BF)
    chips = tm // 2
    part = lax.all_to_all(
        part.reshape(chips, width // cams // chips, CW), "tm", 0, 0, tiled=True, axis_index_groups=same_core
    )
    part = jnp.sum(part.astype(F32), axis=0)
    final = width // cams // tm
    mine = lax.dynamic_slice_in_dim(part, core * final, final, 0)
    theirs = lax.ppermute(lax.dynamic_slice_in_dim(part, (1 - core) * final, final, 0), "tm", swap)
    grad_out_weight = jnp.concatenate(
        [jnp.where(core == 0, mine, theirs), jnp.where(core == 0, theirs, mine)], axis=1
    )

    codes = jnp.arange(act_table.shape[1])
    one_hot = (actions[:, :, None] == codes[None, None, :]).astype(BF).reshape(frames, -1)
    action_sum = jnp.dot(one_hot, act_table.reshape(-1, width), preferred_element_type=F32)

    half_weight = [pltpu.VMEM((CW, width), BF), pltpu.SemaphoreType.DMA((tm // 2,))]
    (view_back,) = call(
        functools.partial(view_backward_kernel, tm),
        [((rows, 4 * CW), BF)],
        [SM] + [VM] * 3 + [ANY] * 2,
        me, view_x, kept_view, prob_view, w_own, w_other,
        scratch=half_weight,
    )
    returned = call(
        functools.partial(time_backward_kernel, tm),
        [((block, 4 * CW), BF)] * GROUP + [((block, 2 * CW), BF)] * GROUP,
        [SM] + [VM] * (2 * GROUP + 2) + [ANY] * 2,
        me, *time_x, *prev, kept_time, prob_time, w_own, w_other,
        scratch=half_weight,
    )
    view_back = lax.all_to_all(view_back, "cam", 0, 0, tiled=True)
    time_back = [returned[0]] + [lax.ppermute(returned[d], "tm", within[d]) for d in range(1, GROUP)]
    back = [lax.ppermute(returned[GROUP + d], "tm", inward[d]) for d in range(GROUP)]
    outs = call(
        functools.partial(finish_kernel, tm),
        [((rows, width), BF)] * 4,
        [SM, VM] + [ANY] * 2 + [VM] * (2 * GROUP + 1),
        me, view_back, w_own, w_other, action_sum, *time_back, *back,
        scratch=[pltpu.VMEM((width, width), BF), pltpu.SemaphoreType.DMA((tm,))],
    )
    return tuple(a.reshape(1, frames, tokens, width) for a in outs) + (grad_out_weight,)


def solution(mesh):
    in_specs = (
        P("cam", "tm", None, None),
        P("cam", "tm", None, None),
        P("cam", "tm", None, None),
        P("cam", "tm"),
        P(),
        P("tm", None),
        P(),
        P("tm", None),
        P("cam", "tm", None, None),
    )
    out_specs = (
        P("cam", "tm", None, None),
        P("cam", "tm", None, None),
        P("cam", "tm", None, None),
        P("cam", "tm", None, None),
        P(("cam", "tm"), None),
    )
    return jax.shard_map(shards, mesh=mesh, in_specs=in_specs, out_specs=out_specs, check_vma=False)
```

```python
import functools
import math

import jax
import jax.numpy as jnp
from jax import lax
from jax.experimental import pallas as pl
from jax.experimental.pallas import tpu as pltpu
from jax.sharding import PartitionSpec as P

HC = 12
HT = 12
HD = 64
WIN = 64
CW = HC * HD
GROUP = 4
SCALE = HD ** (-0.5)
BF = jnp.bfloat16
F32 = jnp.float32
PAIRS = HC // 2
VM = pl.BlockSpec(memory_space=pltpu.VMEM)
ANY = pl.BlockSpec(memory_space=pl.ANY)
SM = pl.BlockSpec(memory_space=pltpu.SMEM)


def params():
    return pltpu.CompilerParams(vmem_limit_bytes=56 * 1024 * 1024)


def iota(shape, dim):
    return lax.broadcasted_iota(jnp.int32, shape, dim)


def dot_nt(a, b):
    return lax.dot_general(a, b, (((1,), (1,)), ((), ())), preferred_element_type=F32)


def dot_tn(a, b):
    return lax.dot_general(a, b, (((0,), (0,)), ((), ())), preferred_element_type=F32)


def dot_nn(a, b):
    return jnp.dot(a, b, preferred_element_type=F32)


def split_pair(rows):
    low = iota(rows.shape, 1) < HD
    zero = jnp.zeros_like(rows)
    return jnp.concatenate([jnp.where(low, rows, zero), jnp.where(low, zero, rows)], axis=0)


def join_pair(rows):
    count = rows.shape[0] // 2
    low = iota((count, rows.shape[1]), 1) < HD
    return jnp.where(low, rows[:count], rows[count:])


def softmax_pair(q, k, mask):
    scores = dot_nt(split_pair(q), k) * SCALE
    scores = jnp.where(mask, scores, -jnp.inf)
    largest = jnp.max(scores, axis=1, keepdims=True)
    e = jnp.exp(scores - largest)
    return e / jnp.sum(e, axis=1, keepdims=True)


def pack_kernel(me, valid, q, k, v, ct, view_ref, *rest):
    own_refs, kv_refs, (held, sems) = rest[:GROUP], rest[GROUP : 2 * GROUP], rest[2 * GROUP :]
    copies = [pltpu.make_async_copy(ref, held.at[i], sems.at[i]) for i, ref in enumerate((q, k, v, ct))]
    for copy in copies:
        copy.start()
    rows = q.shape[0]
    frames = rows // 8
    block = 2 * frames
    row = iota((rows, rows), 0)
    col = iota((rows, rows), 1)
    member = (row // block) ^ me[0]
    source = ((row // 2) % frames) * 8 + 2 * member + row % 2
    perm = jnp.where(col == source, 1.0, 0.0).astype(BF)
    frame = iota((rows, 128), 0) // 8
    flags = jnp.zeros((rows, 128), F32)
    for f in range(frames):
        flags = jnp.where(frame == f, valid[0, f].astype(F32), flags)
    view_ref[:, 5 * CW :] = jnp.where(flags > 0.5, 1.0, 0.0).astype(BF)
    for i in range(4):
        copies[i].wait()
        if i < 3:
            part = slice(i * CW, (i + 1) * CW)
            view_ref[:, part] = held[i, :, :CW]
            moved = dot_nn(perm, held[i, :, CW:]).astype(BF)
        else:
            part = slice(3 * CW, 5 * CW)
            view_ref[:, part] = held[i]
            moved = dot_nn(perm, held[i]).astype(BF)
        for d in range(GROUP):
            own_refs[d][:, part] = moved[d * block : (d + 1) * block]
            if i in (1, 2):
                kv_refs[d][:, (i - 1) * CW : i * CW] = moved[d * block : (d + 1) * block]


def view_mask(flags):
    rows = flags.shape[0]
    pick = jnp.where(iota((8, 128), 1) == 0, 1.0, 0.0).astype(BF)
    valid_row = dot_nt(pick, flags)[:1]
    r = iota((2 * rows, rows), 0) % rows
    c = iota((2 * rows, rows), 1)
    same_frame = ((r // 8) % 2) == ((c // 8) % 2)
    return same_frame & ((valid_row > 0.5) | (r // 16 == c // 16))


def keep_for_weight(attn, ct, core, own_ref, send_ref):
    own_ref[:, :CW] = attn
    send_ref[:, :CW] = attn
    own_ref[:, CW:] = jnp.where(core == 0, ct[:, :CW], ct[:, CW:])
    send_ref[:, CW:] = jnp.where(core == 0, ct[:, CW:], ct[:, :CW])


def view_forward_kernel(me, x, own_ref, send_ref, prob_ref):
    mask = view_mask(x[:, 5 * CW :])
    attn = []
    for j in range(PAIRS):
        q = x[:, 128 * j : 128 * (j + 1)]
        k = x[:, CW + 128 * j : CW + 128 * (j + 1)]
        v = x[:, 2 * CW + 128 * j : 2 * CW + 128 * (j + 1)]
        prob = softmax_pair(q, k, mask)
        prob_ref[j] = prob
        attn.append(join_pair(dot_nn(prob.astype(BF), v)).astype(BF))
    keep_for_weight(jnp.concatenate(attn, axis=1), x[:, 3 * CW : 5 * CW], me[0] % 2, own_ref, send_ref)


def rows_of(refs, columns):
    return jnp.concatenate([ref[:, columns] for ref in refs], axis=0)


def time_forward_kernel(windows, me, block, *refs):
    x, prev, (own_ref, send_ref, prob_ref) = refs[:GROUP], refs[GROUP : 2 * GROUP], refs[2 * GROUP :]
    size = x[0].shape[0]
    rows = GROUP * size
    r = iota((2 * rows, 2 * rows), 0)
    c = iota((2 * rows, 2 * rows), 1)
    second = r >= rows

    def frame_of(row):
        return ((row // size) ^ me[0]) * (size // 2) + (row % size) // 2

    key_frame = frame_of(c % rows) - jnp.where(c < rows, rows // 2, 0)
    gap = frame_of(r % rows) - key_frame
    base = (r % 2 == c % 2) & (gap >= 0) & ((key_frame >= 0) | (block[0] > 0))
    attn = []
    for j in range(PAIRS):
        at = [slice(i * CW + 128 * j, i * CW + 128 * (j + 1)) for i in range(3)]
        k = jnp.concatenate([rows_of(prev, at[0]), rows_of(x, at[1])], axis=0)
        v = jnp.concatenate([rows_of(prev, at[1]), rows_of(x, at[2])], axis=0)
        limit = jnp.where(second, windows[2 * j + 1], windows[2 * j])
        prob = softmax_pair(rows_of(x, at[0]), k, base & (gap < limit))
        prob_ref[j] = prob
        attn.append(join_pair(dot_nn(prob.astype(BF), v)).astype(BF))
    keep_for_weight(
        jnp.concatenate(attn, axis=1), rows_of(x, slice(3 * CW, 5 * CW)), me[0] % 2, own_ref, send_ref
    )


def weight_kernel(scale, own_view, other_view, own_time, other_time, out_ref):
    for i, (own, other) in enumerate(((own_view, other_view), (own_time, other_time))):
        left = jnp.concatenate([own[:, :CW], other[:, :CW]], axis=0)
        right = jnp.concatenate([own[:, CW:], other[:, CW:]], axis=0)
        out_ref[i * CW : (i + 1) * CW, :] = (dot_tn(left, right) * scale).astype(BF)


def fetch_weight(me, own, others, held, sem, first, count):
    size = held.shape[0] // (4 * count)
    core, y = me[0] % 2, me[0] // 2
    copies = []
    for z in range(count):
        other = others[z * len(others) // count]
        for e in range(2):
            for n, (which, ref, place) in enumerate(
                ((core, own, 2 * (first + z) + e), (1 - core, other, 2 * (z % (count // len(others))) + e))
            ):
                start = pl.multiple_of((4 * z + 2 * (y ^ e) + which) * size, 16)
                copies.append(
                    pltpu.make_async_copy(
                        ref.at[pl.ds(place * size, size)],
                        held.at[pl.ds(start, size)],
                        sem.at[4 * z + 2 * e + n],
                    )
                )
    for copy in copies:
        copy.start()
    return copies


def backward_pair(q, k, v, g, prob):
    g2 = split_pair(g)
    grad_prob = dot_nt(g2, v)
    total = jnp.sum(prob * grad_prob, axis=1, keepdims=True)
    grad_scores = (prob * (grad_prob - total)).astype(BF)
    dq = join_pair(dot_nn(grad_scores, k)) * SCALE
    dk = dot_tn(grad_scores, split_pair(q)) * SCALE
    dv = dot_tn(prob.astype(BF), g2)
    return dq, dk, dv


def view_backward_kernel(depth, me, cam, x, kept, prob_ref, w_own, w_other, *rest):
    out_refs, (held, w, sem) = rest[:-3], rest[-3:]
    copies = fetch_weight(me, w_own, (w_other,), w, sem, 0, depth // 2)
    held[:, :CW] = kept[:, :CW]
    for copy in copies:
        copy.wait()
    grad = dot_nt(x[:, 3 * CW : 5 * CW], w[...]).astype(BF)
    for j in range(PAIRS):
        at = [slice(i * CW + 128 * j, i * CW + 128 * (j + 1)) for i in range(4)]
        dq, dk, dv = backward_pair(x[:, at[0]], x[:, at[1]], x[:, at[2]], grad[:, at[0]], prob_ref[j])
        held[:, at[1]] = dq.astype(BF)
        held[:, at[2]] = dk.astype(BF)
        held[:, at[3]] = dv.astype(BF)
    size = held.shape[0] // len(out_refs)
    for d, out in enumerate(out_refs):
        out[...] = held[pl.ds(pl.multiple_of((cam[0] ^ d) * size, size), size), :]


def time_backward_kernel(depth, me, *refs):
    x, prev = refs[:GROUP], refs[GROUP : 2 * GROUP]
    kept, prob_ref, w_own, w_other = refs[2 * GROUP : 2 * GROUP + 4]
    out_refs = refs[2 * GROUP + 4 : 3 * GROUP + 4]
    back_refs = refs[3 * GROUP + 4 : 4 * GROUP + 4]
    w, sem = refs[4 * GROUP + 4 :]
    copies = fetch_weight(me, w_own, (w_other,), w, sem, depth // 2, depth // 2)
    size = x[0].shape[0]
    rows = GROUP * size

    def store(out, columns, value):
        value = value.astype(BF)
        for d in range(GROUP):
            out[d][:, columns] = value[d * size : (d + 1) * size]

    store(out_refs, slice(0, CW), kept[:, :CW])
    for copy in copies:
        copy.wait()
    grad = dot_nt(rows_of(x, slice(3 * CW, 5 * CW)), w[...]).astype(BF)
    for j in range(PAIRS):
        at = [slice(i * CW + 128 * j, i * CW + 128 * (j + 1)) for i in range(4)]
        k = jnp.concatenate([rows_of(prev, at[0]), rows_of(x, at[1])], axis=0)
        v = jnp.concatenate([rows_of(prev, at[1]), rows_of(x, at[2])], axis=0)
        dq, dk, dv = backward_pair(rows_of(x, at[0]), k, v, grad[:, at[0]], prob_ref[j])
        store(out_refs, at[1], dq)
        store(back_refs, at[0], dk[:rows])
        store(out_refs, at[2], dk[rows:])
        store(back_refs, at[1], dv[:rows])
        store(out_refs, at[3], dv[rows:])


def finish_kernel(depth, cams, me, cam, w_own, w_view, w_time, action, *refs):
    time, back, blocks = refs[:GROUP], refs[GROUP : 2 * GROUP], refs[2 * GROUP : 2 * GROUP + cams]
    pred_ref, dq_ref, dk_ref, dv_ref, view, w, sem = refs[2 * GROUP + cams :]
    copies = fetch_weight(me, w_own, (w_view, w_time), w, sem, 0, depth)
    size = blocks[0].shape[0]
    for d, part in enumerate(blocks):
        view[pl.ds(pl.multiple_of((cam[0] ^ d) * size, size), size), :] = part[...]
    rows = view.shape[0]
    frames = rows // 8
    row = iota((rows, rows), 0)
    col = iota((rows, rows), 1)
    source = (((row // 2) % GROUP) ^ me[0]) * 2 * frames + (row // 8) * 2 + row % 2
    perm = jnp.where(col == source, 1.0, 0.0).astype(BF)
    for i, ref in enumerate((dq_ref, dk_ref, dv_ref), 1):
        part = slice(i * CW, (i + 1) * CW)
        rows_time = rows_of(time, part)
        if i > 1:
            returned = rows_of(back, slice((i - 2) * CW, (i - 1) * CW))
            rows_time = (rows_time.astype(F32) + returned.astype(F32)).astype(BF)
        ref[:, :CW] = view[:, part]
        ref[:, CW:] = dot_nn(perm, rows_time).astype(BF)
    attn_time = dot_nn(perm, rows_of(time, slice(0, CW))).astype(BF)
    for copy in copies:
        copy.wait()
    mixed = dot_nn(view[:, :CW], w[:CW]) + dot_nn(attn_time, w[CW:])
    total = mixed.reshape(frames, 8, 2 * CW) + action[...][:, None, :]
    pred_ref[...] = total.reshape(rows, 2 * CW).astype(BF)


def whole(shape):
    return pl.BlockSpec(shape, lambda *at: (0,) * len(shape))


def call(kernel, outs, specs, *args, scratch=()):
    specs = [whole(arg.shape) if spec is VM else spec for spec, arg in zip(specs, args)]
    return list(pl.pallas_call(
        kernel,
        out_shape=[jax.ShapeDtypeStruct(shape, kind) for shape, kind in outs],
        in_specs=specs,
        out_specs=[whole(shape) for shape, _ in outs],
        grid=(1,),
        scratch_shapes=list(scratch),
        compiler_params=params(),
    )(*args))


def shards(queries, keys, values, cam_valid, windows, actions, act_table, w_out, cotangent):
    _, frames, tokens, width = queries.shape
    rows = frames * tokens
    block = rows // GROUP
    cams = lax.axis_size("cam")
    tm = lax.axis_size("tm")
    at_tm = lax.axis_index("tm")
    core = at_tm % 2
    me = (at_tm % GROUP).reshape(1)
    group = (at_tm // GROUP).reshape(1)
    same_core = [[2 * i + j for i in range(tm // 2)] for j in range(2)]
    swap = [(i, i ^ 1) for i in range(tm)]
    onward = [[(i, (i + GROUP) ^ d) for i in range(tm - GROUP)] for d in range(GROUP)]
    inward = [[((i + GROUP) ^ d, i) for i in range(tm - GROUP)] for d in range(GROUP)]
    within = [[(i, i ^ d) for i in range(tm)] for d in range(GROUP)]

    depth = tm // GROUP
    along_z = [[GROUP * i + j for i in range(depth)] for j in range(GROUP)]
    beside = [(i, i ^ (tm + 2)) for i in range(cams * tm)]
    w_both = jnp.concatenate([w_out, lax.ppermute(w_out, ("cam", "tm"), beside)], axis=0)
    w_own = lax.all_gather(w_both, "tm", axis=0, tiled=True, axis_index_groups=along_z)
    w_view = lax.ppermute(w_own[:CW // 2], "tm", swap)
    w_time = lax.ppermute(w_own[CW // 2:], "tm", swap)
    q, k, v, ct = (a.reshape(rows, width) for a in (queries, keys, values, cotangent))
    packed = call(
        pack_kernel,
        [((rows, 5 * CW + 128), BF)] + [((block, 5 * CW), BF)] * GROUP + [((block, 2 * CW), BF)] * GROUP,
        [SM, SM] + [ANY] * 4,
        me, cam_valid, q, k, v, ct,
        scratch=[pltpu.VMEM((4, rows, width), BF), pltpu.SemaphoreType.DMA((4,))],
    )
    view_send, time_send, kv_send = packed[0], packed[1 : GROUP + 1], packed[GROUP + 1 :]
    view_x = lax.all_to_all(view_send, "cam", 0, 0, tiled=True)
    time_x = [time_send[0]] + [lax.ppermute(time_send[d], "tm", within[d]) for d in range(1, GROUP)]
    prev = [lax.ppermute(kv_send[d], "tm", onward[d]) for d in range(GROUP)]

    codes = jnp.arange(act_table.shape[1])
    one_hot = (actions[:, :, None] == codes[None, None, :]).astype(BF).reshape(frames, -1)
    action_sum = jnp.dot(one_hot, act_table.reshape(-1, width), preferred_element_type=F32)
    view_x, action_sum = lax.optimization_barrier((view_x, action_sum))

    kept_view, view_swap, prob_view = call(
        view_forward_kernel,
        [((rows, 2 * CW), BF)] * 2 + [((PAIRS, 2 * rows, rows), F32)],
        [SM, VM],
        me, view_x,
    )
    kept_time, time_swap, prob_time = call(
        time_forward_kernel,
        [((rows, 2 * CW), BF)] * 2 + [((PAIRS, 2 * rows, 2 * rows), F32)],
        [SM] * 3 + [VM] * (2 * GROUP),
        windows, me, group, *time_x, *prev,
    )

    view_swap = lax.ppermute(view_swap, "tm", swap)
    time_swap = lax.ppermute(time_swap, "tm", swap)
    grad_norm = 1.0 / math.sqrt(cams * tm * rows)
    (part,) = call(
        functools.partial(weight_kernel, grad_norm),
        [((width, CW), BF)],
        [VM] * 4,
        kept_view, view_swap, kept_time, time_swap,
    )
    part = lax.all_to_all(part.reshape(cams, width // cams, CW), "cam", 0, 0, tiled=True)
    half_weight = [pltpu.VMEM((CW, width), BF), pltpu.SemaphoreType.DMA((tm // 2,))]
    cam = lax.axis_index("cam").reshape(1)
    share = rows // cams
    view_out = call(
        functools.partial(view_backward_kernel, depth),
        [((share, 4 * CW), BF)] * cams,
        [SM, SM] + [VM] * 3 + [ANY] * 2,
        me, cam, view_x, kept_view, prob_view, w_own, w_view,
        scratch=[pltpu.VMEM((rows, 4 * CW), BF)] + half_weight,
    )
    returned = call(
        functools.partial(time_backward_kernel, depth),
        [((block, 4 * CW), BF)] * GROUP + [((block, 2 * CW), BF)] * GROUP,
        [SM] + [VM] * (2 * GROUP + 2) + [ANY] * 2,
        me, *time_x, *prev, kept_time, prob_time, w_own, w_time,
        scratch=half_weight,
    )
    part, view_out[0], returned[0] = lax.optimization_barrier((part, view_out[0], returned[0]))
    part = jnp.sum(part.astype(F32), axis=0).astype(BF)
    chips = tm // 2
    part = lax.all_to_all(
        part.reshape(chips, width // cams // chips, CW), "tm", 0, 0, tiled=True, axis_index_groups=same_core
    )
    part = jnp.sum(part.astype(F32), axis=0)
    final = width // cams // tm
    mine = lax.dynamic_slice_in_dim(part, core * final, final, 0)
    theirs = lax.ppermute(lax.dynamic_slice_in_dim(part, (1 - core) * final, final, 0), "tm", swap)
    grad_out_weight = jnp.concatenate(
        [jnp.where(core == 0, mine, theirs), jnp.where(core == 0, theirs, mine)], axis=1
    )

    view_back = [view_out[0]] + [
        lax.ppermute(view_out[d], "cam", [(i, i ^ d) for i in range(cams)]) for d in range(1, cams)
    ]
    time_back = [returned[0]] + [lax.ppermute(returned[d], "tm", within[d]) for d in range(1, GROUP)]
    back = [lax.ppermute(returned[GROUP + d], "tm", inward[d]) for d in range(GROUP)]
    outs = call(
        functools.partial(finish_kernel, depth, cams),
        [((rows, width), BF)] * 4,
        [SM, SM] + [ANY] * 3 + [VM] * (2 * GROUP + 1 + cams),
        me, cam, w_own, w_view, w_time, action_sum, *time_back, *back, *view_back,
        scratch=[
            pltpu.VMEM((rows, 4 * CW), BF),
            pltpu.VMEM((width, width), BF),
            pltpu.SemaphoreType.DMA((tm,)),
        ],
    )
    return tuple(a.reshape(1, frames, tokens, width) for a in outs) + (grad_out_weight,)


def solution(mesh):
    in_specs = (
        P("cam", "tm", None, None),
        P("cam", "tm", None, None),
        P("cam", "tm", None, None),
        P("cam", "tm"),
        P(),
        P("tm", None),
        P(),
        P("tm", None),
        P("cam", "tm", None, None),
    )
    out_specs = (
        P("cam", "tm", None, None),
        P("cam", "tm", None, None),
        P("cam", "tm", None, None),
        P("cam", "tm", None, None),
        P(("cam", "tm"), None),
    )
    return jax.shard_map(shards, mesh=mesh, in_specs=in_specs, out_specs=out_specs, check_vma=False)
```

```python
import functools
import math

import jax
import jax.numpy as jnp
from jax import lax
from jax.experimental import pallas as pl
from jax.experimental.pallas import tpu as pltpu
from jax.sharding import PartitionSpec as P

HC = 12
HT = 12
HD = 64
WIN = 64
CW = HC * HD
GROUP = 4
PAIR = 2
SCALE = HD ** (-0.5)
BF = jnp.bfloat16
F32 = jnp.float32
PAIRS = HC // 2
VM = pl.BlockSpec(memory_space=pltpu.VMEM)
ANY = pl.BlockSpec(memory_space=pl.ANY)
SM = pl.BlockSpec(memory_space=pltpu.SMEM)


def iota(shape, dim):
    return lax.broadcasted_iota(jnp.int32, shape, dim)


def dot_nt(a, b):
    return lax.dot_general(a, b, (((1,), (1,)), ((), ())), preferred_element_type=F32)


def dot_tn(a, b):
    return lax.dot_general(a, b, (((0,), (0,)), ((), ())), preferred_element_type=F32)


def dot_nn(a, b):
    return jnp.dot(a, b, preferred_element_type=F32)


def split_pair(rows):
    low = iota(rows.shape, 1) < HD
    zero = jnp.zeros_like(rows)
    return jnp.concatenate([jnp.where(low, rows, zero), jnp.where(low, zero, rows)], axis=0)


def join_pair(rows):
    count = rows.shape[0] // 2
    low = iota((count, rows.shape[1]), 1) < HD
    return jnp.where(low, rows[:count], rows[count:])


def softmax_pair(q, k, mask):
    scores = dot_nt(split_pair(q), k) * SCALE
    scores = jnp.where(mask, scores, -jnp.inf)
    largest = jnp.max(scores, axis=1, keepdims=True)
    e = jnp.exp(scores - largest)
    return e / jnp.sum(e, axis=1, keepdims=True)


def pack_kernel(me, valid, q, k, v, ct, view_ref, *rest):
    kv_refs, qct_refs, (held, sems) = rest[:PAIR], rest[PAIR : 2 * PAIR], rest[2 * PAIR :]
    copies = [pltpu.make_async_copy(ref, held.at[i], sems.at[i]) for i, ref in enumerate((q, k, v, ct))]
    for copy in copies:
        copy.start()
    rows = q.shape[0]
    frames = rows // 8
    block = 4 * frames
    row = iota((rows, rows), 0)
    col = iota((rows, rows), 1)
    source = ((row // 4) % frames) * 8 + 4 * ((row // block) ^ (me[0] % 2)) + row % 4
    perm = jnp.where(col == source, 1.0, 0.0).astype(BF)
    frame = iota((rows, 128), 0) // 8
    flags = jnp.zeros((rows, 128), F32)
    for f in range(frames):
        flags = jnp.where(frame == f, valid[0, f].astype(F32), flags)
    view_ref[:, 5 * CW :] = jnp.where(flags > 0.5, 1.0, 0.0).astype(BF)
    for i in range(4):
        copies[i].wait()
        if i < 3:
            view_ref[:, i * CW : (i + 1) * CW] = held[i, :, :CW]
            moved = dot_nn(perm, held[i, :, CW:]).astype(BF)
        else:
            view_ref[:, 3 * CW : 5 * CW] = held[i]
            moved = dot_nn(perm, held[i]).astype(BF)
        for d in range(PAIR):
            part = moved[d * block : (d + 1) * block]
            if i in (1, 2):
                kv_refs[d][:, (i - 1) * CW : i * CW] = part
            elif i == 0:
                qct_refs[d][:, :CW] = part
            else:
                qct_refs[d][:, CW:] = part


def view_mask(flags):
    rows = flags.shape[0]
    pick = jnp.where(iota((8, 128), 1) == 0, 1.0, 0.0).astype(BF)
    valid_row = dot_nt(pick, flags)[:1]
    r = iota((2 * rows, rows), 0) % rows
    c = iota((2 * rows, rows), 1)
    same_frame = ((r // 8) % 2) == ((c // 8) % 2)
    return same_frame & ((valid_row > 0.5) | (r // 16 == c // 16))


def keep_for_weight(attn, ct, core, own_ref, send_ref):
    own_ref[:, :CW] = attn
    send_ref[:, :CW] = attn
    own_ref[:, CW:] = jnp.where(core == 0, ct[:, :CW], ct[:, CW:])
    send_ref[:, CW:] = jnp.where(core == 0, ct[:, CW:], ct[:, :CW])


def view_forward_kernel(me, x, own_ref, send_ref, prob_ref):
    mask = view_mask(x[:, 5 * CW :])
    attn = []
    for j in range(PAIRS):
        q = x[:, 128 * j : 128 * (j + 1)]
        k = x[:, CW + 128 * j : CW + 128 * (j + 1)]
        v = x[:, 2 * CW + 128 * j : 2 * CW + 128 * (j + 1)]
        prob = softmax_pair(q, k, mask)
        prob_ref[j] = prob
        attn.append(join_pair(dot_nn(prob.astype(BF), v)).astype(BF))
    keep_for_weight(jnp.concatenate(attn, axis=1), x[:, 3 * CW : 5 * CW], me[0] % 2, own_ref, send_ref)


def rows_of(refs, columns):
    return jnp.concatenate([ref[:, columns] for ref in refs], axis=0)


def time_forward_kernel(windows, me, pair, q0, q1, far, near, own, own_ref, send_ref, prob_ref):
    qct, kv = (q0, q1), (far, near, own)
    size = q0.shape[0]
    rows = PAIR * size
    shape = (2 * rows, 3 * rows)
    r = iota(shape, 0)
    c = iota(shape, 1)
    second = r >= rows
    core = me[0] % 2
    span = size // 2

    def frame_of(row):
        return ((row // size) ^ core) * (size // 4) + (row % size) // 4

    key_frame = frame_of(c % rows) + span * (c // rows) - 2 * span
    gap = frame_of(r % rows) - key_frame
    base = (r % 4 == c % 4) & (gap >= 0) & (key_frame + span * pair[0] >= 0)
    attn = []
    for j in range(PAIRS):
        at = [slice(i * CW + 128 * j, i * CW + 128 * (j + 1)) for i in range(2)]
        limit = jnp.where(second, windows[2 * j + 1], windows[2 * j])
        prob = softmax_pair(rows_of(qct, at[0]), rows_of(kv, at[0]), base & (gap < limit))
        prob_ref[j] = prob
        attn.append(join_pair(dot_nn(prob.astype(BF), rows_of(kv, at[1]))).astype(BF))
    keep_for_weight(jnp.concatenate(attn, axis=1), rows_of(qct, slice(CW, 3 * CW)), core, own_ref, send_ref)


def weight_kernel(scale, own_view, other_view, own_time, other_time, out_ref):
    for i, (own, other) in enumerate(((own_view, other_view), (own_time, other_time))):
        left = jnp.concatenate([own[:, :CW], other[:, :CW]], axis=0)
        right = jnp.concatenate([own[:, CW:], other[:, CW:]], axis=0)
        out_ref[i * CW : (i + 1) * CW, :] = (dot_tn(left, right) * scale).astype(BF)


def fetch_weight(me, own, others, held, sem, first, count):
    size = held.shape[0] // (4 * count)
    core, y = me[0] % 2, me[0] // 2
    copies = []
    for z in range(count):
        other = others[z * len(others) // count]
        for e in range(2):
            for n, (which, ref, place) in enumerate(
                ((core, own, 2 * (first + z) + e), (1 - core, other, 2 * (z % (count // len(others))) + e))
            ):
                start = pl.multiple_of((4 * z + 2 * (y ^ e) + which) * size, 16)
                copies.append(
                    pltpu.make_async_copy(
                        ref.at[pl.ds(place * size, size)],
                        held.at[pl.ds(start, size)],
                        sem.at[4 * z + 2 * e + n],
                    )
                )
    for copy in copies:
        copy.start()
    return copies


def backward_pair(q, k, v, g, prob):
    g2 = split_pair(g)
    grad_prob = dot_nt(g2, v)
    total = jnp.sum(prob * grad_prob, axis=1, keepdims=True)
    grad_scores = (prob * (grad_prob - total)).astype(BF)
    dq = join_pair(dot_nn(grad_scores, k)) * SCALE
    dk = dot_tn(grad_scores, split_pair(q)) * SCALE
    dv = dot_tn(prob.astype(BF), g2)
    return dq, dk, dv


def view_backward_kernel(depth, me, x, kept, prob_ref, w_own, w_other, out_ref, w, sem):
    copies = fetch_weight(me, w_own, (w_other,), w, sem, 0, depth // 2)
    out_ref[:, :CW] = kept[:, :CW]
    for copy in copies:
        copy.wait()
    grad = dot_nt(x[:, 3 * CW : 5 * CW], w[...]).astype(BF)
    for j in range(PAIRS):
        at = [slice(i * CW + 128 * j, i * CW + 128 * (j + 1)) for i in range(4)]
        dq, dk, dv = backward_pair(x[:, at[0]], x[:, at[1]], x[:, at[2]], grad[:, at[0]], prob_ref[j])
        out_ref[:, at[1]] = dq.astype(BF)
        out_ref[:, at[2]] = dk.astype(BF)
        out_ref[:, at[3]] = dv.astype(BF)


def time_backward_kernel(depth, me, q0, q1, far, near, own, prob_ref, w_own, w_other, *rest):
    dq_ref, own_ref, near_ref, far_ref, w, sem = rest
    qct, kv = (q0, q1), (far, near, own)
    copies = fetch_weight(me, w_own, (w_other,), w, sem, depth // 2, depth // 2)
    rows = PAIR * q0.shape[0]
    for copy in copies:
        copy.wait()
    grad = dot_nt(rows_of(qct, slice(CW, 3 * CW)), w[...]).astype(BF)
    for j in range(PAIRS):
        at = [slice(i * CW + 128 * j, i * CW + 128 * (j + 1)) for i in range(2)]
        dq, dk, dv = backward_pair(
            rows_of(qct, at[0]), rows_of(kv, at[0]), rows_of(kv, at[1]), grad[:, at[0]], prob_ref[j]
        )
        dq_ref[:, at[0]] = dq.astype(BF)
        for part, value in zip(at, (dk, dv)):
            far_ref[:, part] = value[:rows].astype(BF)
            near_ref[:, part] = value[rows : 2 * rows].astype(BF)
            own_ref[:, part] = value[2 * rows :]


def time_sum_kernel(kept, dq, own, near, far, *outs):
    size = outs[0].shape[0]
    for d, out in enumerate(outs):
        part = slice(d * size, (d + 1) * size)
        out[:, :CW] = kept[part, :CW]
        out[:, CW : 2 * CW] = dq[part]
        out[:, 2 * CW :] = (own[part] + near[part].astype(F32) + far[part].astype(F32)).astype(BF)


def action_kernel(actions, table, out_ref):
    total = None
    for d in range(table.shape[0]):
        codes = iota((actions.shape[0], table.shape[1]), 1)
        one_hot = jnp.where(actions[:, d : d + 1] == codes, 1.0, 0.0).astype(BF)
        term = dot_nn(one_hot, table[d])
        total = term if total is None else total + term
    out_ref[...] = total


def camera_sum_kernel(parts, out_ref, held):
    total = parts[0].astype(F32)
    for i in range(1, parts.shape[0]):
        total = total + parts[i].astype(F32)
    held[...] = total
    size = out_ref.shape[1]
    for i in range(out_ref.shape[0]):
        out_ref[i] = held[i * size : (i + 1) * size, :].astype(BF)


def finish_kernel(depth, me, w_own, w_view, w_time, action, t0, t1, view, *rest):
    time = (t0, t1)
    pred_ref, dq_ref, dk_ref, dv_ref, w, sem = rest
    copies = fetch_weight(me, w_own, (w_view, w_time), w, sem, 0, depth)
    rows = view.shape[0]
    frames = rows // 8
    row = iota((rows, rows), 0)
    col = iota((rows, rows), 1)
    source = (((row % 8) // 4) ^ (me[0] % 2)) * 4 * frames + (row // 8) * 4 + row % 4
    perm = jnp.where(col == source, 1.0, 0.0).astype(BF)
    for i, ref in enumerate((dq_ref, dk_ref, dv_ref), 1):
        part = slice(i * CW, (i + 1) * CW)
        ref[:, :CW] = view[:, part]
        ref[:, CW:] = dot_nn(perm, rows_of(time, part)).astype(BF)
    attn_time = dot_nn(perm, rows_of(time, slice(0, CW))).astype(BF)
    for copy in copies:
        copy.wait()
    mixed = dot_nn(view[:, :CW], w[:CW]) + dot_nn(attn_time, w[CW:])
    total = mixed.reshape(frames, 8, 2 * CW) + action[...][:, None, :]
    pred_ref[...] = total.reshape(rows, 2 * CW).astype(BF)


def call(kernel, outs, specs, *args, scratch=()):
    return list(
        pl.pallas_call(
            kernel,
            out_shape=[jax.ShapeDtypeStruct(shape, kind) for shape, kind in outs],
            in_specs=specs,
            out_specs=[VM] * len(outs),
            scratch_shapes=list(scratch),
            compiler_params=pltpu.CompilerParams(vmem_limit_bytes=20 * 1024 * 1024),
        )(*args)
    )


def shards(queries, keys, values, cam_valid, windows, actions, act_table, w_out, cotangent):
    _, frames, tokens, width = queries.shape
    rows = frames * tokens
    block = rows // PAIR
    cams = lax.axis_size("cam")
    tm = lax.axis_size("tm")
    at_tm = lax.axis_index("tm")
    core = at_tm % 2
    me = (at_tm % GROUP).reshape(1)
    pair = (at_tm // PAIR).reshape(1)
    depth = tm // GROUP
    same_core = [[2 * i + j for i in range(tm // 2)] for j in range(2)]
    along_z = [[GROUP * i + j for i in range(depth)] for j in range(GROUP)]
    swap = [(i, i ^ 1) for i in range(tm)]
    beside = [(i, i ^ (tm + 2)) for i in range(cams * tm)]

    w_beside = lax.ppermute(w_out, ("cam", "tm"), beside)
    q, k, v, ct = (a.reshape(rows, width) for a in (queries, keys, values, cotangent))
    packed = call(
        pack_kernel,
        [((rows, 5 * CW + 128), BF)] + [((block, 2 * CW), BF)] * PAIR + [((block, 3 * CW), BF)] * PAIR,
        [SM, SM] + [ANY] * 4,
        me, cam_valid, q, k, v, ct,
        scratch=[pltpu.VMEM((4, rows, width), BF), pltpu.SemaphoreType.DMA((4,))],
    )
    view_send, kv, qct = packed[0], packed[1 : PAIR + 1], packed[PAIR + 1 :]
    w_beside, view_send = lax.optimization_barrier((w_beside, view_send))
    w_both = jnp.concatenate([w_out, w_beside], axis=0)
    w_own = lax.all_gather(w_both, "tm", axis=0, tiled=True, axis_index_groups=along_z)
    view_x = lax.all_to_all(view_send, "cam", 0, 0, tiled=True)
    own = jnp.concatenate([kv[0], lax.ppermute(kv[1], "tm", swap)], axis=0)
    near = lax.ppermute(own, "tm", [(i, i + 2) for i in range(tm - 2)])
    far = lax.ppermute(own, "tm", [(i, i + 4) for i in range(tm - 4)])
    q0, q1 = qct[0], lax.ppermute(qct[1], "tm", swap)

    (action_sum,) = call(action_kernel, [((frames, width), F32)], [VM] * 2, actions, act_table)
    view_x, action_sum = lax.optimization_barrier((view_x, action_sum))
    kept_view, view_swap, prob_view = call(
        view_forward_kernel,
        [((rows, 2 * CW), BF)] * 2 + [((PAIRS, 2 * rows, rows), F32)],
        [SM, VM],
        me, view_x,
    )
    kept_time, time_swap, prob_time = call(
        time_forward_kernel,
        [((rows, 2 * CW), BF)] * 2 + [((PAIRS, 2 * rows, 3 * rows), F32)],
        [SM] * 3 + [VM] * 5,
        windows, me, pair, q0, q1, far, near, own,
    )

    view_swap = lax.ppermute(view_swap, "tm", swap)
    time_swap = lax.ppermute(time_swap, "tm", swap)
    grad_norm = 1.0 / math.sqrt(cams * tm * rows)
    (part,) = call(
        functools.partial(weight_kernel, grad_norm),
        [((width, CW), BF)],
        [VM] * 4,
        kept_view, view_swap, kept_time, time_swap,
    )
    part = lax.all_to_all(part.reshape(cams, width // cams, CW), "cam", 0, 0, tiled=True)

    w_view = lax.ppermute(w_own[: CW // 2], "tm", swap)
    w_time = lax.ppermute(w_own[CW // 2 :], "tm", swap)
    half_weight = [pltpu.VMEM((CW, width), BF), pltpu.SemaphoreType.DMA((tm // 2,))]
    (view_out,) = call(
        functools.partial(view_backward_kernel, depth),
        [((rows, 4 * CW), BF)],
        [SM] + [VM] * 3 + [ANY] * 2,
        me, view_x, kept_view, prob_view, w_own, w_view,
        scratch=half_weight,
    )
    q0, view_out = lax.optimization_barrier((q0, view_out))
    view_back = lax.all_to_all(view_out, "cam", 0, 0, tiled=True)
    dq_time, own_grad, near_grad, far_grad = call(
        functools.partial(time_backward_kernel, depth),
        [((rows, CW), BF), ((rows, 2 * CW), F32), ((rows, 2 * CW), BF), ((rows, 2 * CW), BF)],
        [SM] + [VM] * 6 + [ANY] * 2,
        me, q0, q1, far, near, own, prob_time, w_own, w_time,
        scratch=half_weight,
    )
    part, near_grad = lax.optimization_barrier((part, near_grad))
    near_grad = lax.ppermute(near_grad, "tm", [(i + 2, i) for i in range(tm - 2)])
    far_grad = lax.ppermute(far_grad, "tm", [(i + 4, i) for i in range(tm - 4)])

    chips = tm // 2
    (part,) = call(
        camera_sum_kernel,
        [((chips, width // cams // chips, CW), BF)],
        [VM],
        part,
        scratch=[pltpu.VMEM((width // cams, CW), F32)],
    )
    part = lax.all_to_all(part, "tm", 0, 0, tiled=True, axis_index_groups=same_core)
    part = jnp.sum(part.astype(F32), axis=0)
    final = width // cams // tm
    mine = lax.dynamic_slice_in_dim(part, core * final, final, 0)
    theirs = lax.ppermute(lax.dynamic_slice_in_dim(part, (1 - core) * final, final, 0), "tm", swap)
    grad_out_weight = jnp.concatenate(
        [jnp.where(core == 0, mine, theirs), jnp.where(core == 0, theirs, mine)], axis=1
    )

    t0, t1 = call(
        time_sum_kernel, [((block, 4 * CW), BF)] * PAIR, [VM] * 5, kept_time, dq_time, own_grad, near_grad, far_grad
    )
    t1 = lax.ppermute(t1, "tm", swap)
    outs = call(
        functools.partial(finish_kernel, depth),
        [((rows, width), BF)] * 4,
        [SM] + [ANY] * 3 + [VM] * 4,
        me, w_own, w_view, w_time, action_sum, t0, t1, view_back,
        scratch=[pltpu.VMEM((width, width), BF), pltpu.SemaphoreType.DMA((tm,))],
    )
    return tuple(a.reshape(1, frames, tokens, width) for a in outs) + (grad_out_weight,)


def solution(mesh):
    in_specs = (
        P("cam", "tm", None, None),
        P("cam", "tm", None, None),
        P("cam", "tm", None, None),
        P("cam", "tm"),
        P(),
        P("tm", None),
        P(),
        P("tm", None),
        P("cam", "tm", None, None),
    )
    out_specs = (
        P("cam", "tm", None, None),
        P("cam", "tm", None, None),
        P("cam", "tm", None, None),
        P("cam", "tm", None, None),
        P(("cam", "tm"), None),
    )
    return jax.shard_map(shards, mesh=mesh, in_specs=in_specs, out_specs=out_specs, check_vma=False)
```

```python
import functools
import math

import jax
import jax.numpy as jnp
from jax import lax
from jax.experimental import pallas as pl
from jax.experimental.pallas import tpu as pltpu
from jax.sharding import PartitionSpec as P

HC = 12
HT = 12
HD = 64
WIN = 64
CW = HC * HD
GROUP = 4
PAIR = 2
SCALE = HD ** (-0.5)
BF = jnp.bfloat16
F32 = jnp.float32
PAIRS = HC // 2
VM = pl.BlockSpec(memory_space=pltpu.VMEM)
ANY = pl.BlockSpec(memory_space=pl.ANY)
SM = pl.BlockSpec(memory_space=pltpu.SMEM)


def iota(shape, dim):
    return lax.broadcasted_iota(jnp.int32, shape, dim)


def dot_nt(a, b):
    return lax.dot_general(a, b, (((1,), (1,)), ((), ())), preferred_element_type=F32)


def dot_tn(a, b):
    return lax.dot_general(a, b, (((0,), (0,)), ((), ())), preferred_element_type=F32)


def dot_nn(a, b):
    return jnp.dot(a, b, preferred_element_type=F32)


def split_pair(rows):
    low = iota(rows.shape, 1) < HD
    zero = jnp.zeros_like(rows)
    return jnp.concatenate([jnp.where(low, rows, zero), jnp.where(low, zero, rows)], axis=0)


def join_pair(rows):
    count = rows.shape[0] // 2
    low = iota((count, rows.shape[1]), 1) < HD
    return jnp.where(low, rows[:count], rows[count:])


def softmax_pair(q, k, mask):
    scores = dot_nt(split_pair(q), k) * SCALE
    scores = jnp.where(mask, scores, -jnp.inf)
    largest = jnp.max(scores, axis=1, keepdims=True)
    e = jnp.exp(scores - largest)
    return e / jnp.sum(e, axis=1, keepdims=True)


def pack_kernel(me, valid, q, k, v, ct, view_ref, *rest):
    kv_refs, qct_refs, (held, sems) = rest[:PAIR], rest[PAIR : 2 * PAIR], rest[2 * PAIR :]
    copies = [pltpu.make_async_copy(ref, held.at[i], sems.at[i]) for i, ref in enumerate((q, k, v, ct))]
    for copy in copies:
        copy.start()
    rows = q.shape[0]
    frames = rows // 8
    block = 4 * frames
    row = iota((rows, rows), 0)
    col = iota((rows, rows), 1)
    source = ((row // 4) % frames) * 8 + 4 * ((row // block) ^ (me[0] % 2)) + row % 4
    perm = jnp.where(col == source, 1.0, 0.0).astype(BF)
    frame = iota((rows, 128), 0) // 8
    flags = jnp.zeros((rows, 128), F32)
    for f in range(frames):
        flags = jnp.where(frame == f, valid[0, f].astype(F32), flags)
    view_ref[:, 5 * CW :] = jnp.where(flags > 0.5, 1.0, 0.0).astype(BF)
    for i in range(4):
        copies[i].wait()
        if i < 3:
            view_ref[:, i * CW : (i + 1) * CW] = held[i, :, :CW]
            moved = dot_nn(perm, held[i, :, CW:]).astype(BF)
        else:
            view_ref[:, 3 * CW : 5 * CW] = held[i]
            moved = dot_nn(perm, held[i]).astype(BF)
        for d in range(PAIR):
            part = moved[d * block : (d + 1) * block]
            if i in (1, 2):
                kv_refs[d][:, (i - 1) * CW : i * CW] = part
            elif i == 0:
                qct_refs[d][:, :CW] = part
            else:
                qct_refs[d][:, CW:] = part


def view_mask(flags):
    rows = flags.shape[0]
    pick = jnp.where(iota((8, 128), 1) == 0, 1.0, 0.0).astype(BF)
    valid_row = dot_nt(pick, flags)[:1]
    r = iota((2 * rows, rows), 0) % rows
    c = iota((2 * rows, rows), 1)
    same_frame = ((r // 8) % 2) == ((c // 8) % 2)
    return same_frame & ((valid_row > 0.5) | (r // 16 == c // 16))


def keep_for_weight(attn, ct, core, own_ref, send_ref):
    own_ref[:, :CW] = attn
    send_ref[:, :CW] = attn
    own_ref[:, CW:] = jnp.where(core == 0, ct[:, :CW], ct[:, CW:])
    send_ref[:, CW:] = jnp.where(core == 0, ct[:, CW:], ct[:, :CW])


def view_forward_kernel(me, x, own_ref, send_ref, prob_ref):
    mask = view_mask(x[:, 5 * CW :])
    attn = []
    for j in range(PAIRS):
        q = x[:, 128 * j : 128 * (j + 1)]
        k = x[:, CW + 128 * j : CW + 128 * (j + 1)]
        v = x[:, 2 * CW + 128 * j : 2 * CW + 128 * (j + 1)]
        prob = softmax_pair(q, k, mask)
        prob_ref[j] = prob
        attn.append(join_pair(dot_nn(prob.astype(BF), v)).astype(BF))
    keep_for_weight(jnp.concatenate(attn, axis=1), x[:, 3 * CW : 5 * CW], me[0] % 2, own_ref, send_ref)


def rows_of(refs, columns):
    return jnp.concatenate([ref[:, columns] for ref in refs], axis=0)


def time_forward_kernel(windows, me, pair, q0, q1, far, near, own, own_ref, send_ref, prob_ref):
    qct, kv = (q0, q1), (far, near, own)
    size = q0.shape[0]
    rows = PAIR * size
    shape = (2 * rows, 3 * rows)
    r = iota(shape, 0)
    c = iota(shape, 1)
    second = r >= rows
    core = me[0] % 2
    span = size // 2

    def frame_of(row):
        return ((row // size) ^ core) * (size // 4) + (row % size) // 4

    key_frame = frame_of(c % rows) + span * (c // rows) - 2 * span
    gap = frame_of(r % rows) - key_frame
    base = (r % 4 == c % 4) & (gap >= 0) & (key_frame + span * pair[0] >= 0)
    attn = []
    for j in range(PAIRS):
        at = [slice(i * CW + 128 * j, i * CW + 128 * (j + 1)) for i in range(2)]
        limit = jnp.where(second, windows[2 * j + 1], windows[2 * j])
        prob = softmax_pair(rows_of(qct, at[0]), rows_of(kv, at[0]), base & (gap < limit))
        prob_ref[j] = prob
        attn.append(join_pair(dot_nn(prob.astype(BF), rows_of(kv, at[1]))).astype(BF))
    keep_for_weight(jnp.concatenate(attn, axis=1), rows_of(qct, slice(CW, 3 * CW)), core, own_ref, send_ref)


def weight_kernel(scale, own_view, other_view, own_time, other_time, out_ref):
    for i, (own, other) in enumerate(((own_view, other_view), (own_time, other_time))):
        left = jnp.concatenate([own[:, :CW], other[:, :CW]], axis=0)
        right = jnp.concatenate([own[:, CW:], other[:, CW:]], axis=0)
        out_ref[i * CW : (i + 1) * CW, :] = (dot_tn(left, right) * scale).astype(BF)


def fetch_weight(me, z, own, others, held, sem):
    depth = len(own)
    size = own[0].shape[0] // 2
    core, y = me[0] % 2, me[0] // 2
    copies = []
    for i in range(depth):
        place = lax.rem(z[0] + offset(i, depth), depth)
        for n, (which, ref) in enumerate(((core, own[i]), (1 - core, others[i]))):
            for e in range(2):
                start = pl.multiple_of((4 * place + 2 * (y ^ e) + which) * size, 16)
                copies.append(
                    pltpu.make_async_copy(
                        ref.at[pl.ds(e * size, size)], held.at[pl.ds(start, size)], sem.at[4 * i + 2 * n + e]
                    )
                )
    for copy in copies:
        copy.start()
    return copies


def offset(i, depth):
    return (i + 1) // 2 if i % 2 == 0 else depth - (i + 1) // 2


def backward_pair(q, k, v, g, prob):
    g2 = split_pair(g)
    grad_prob = dot_nt(g2, v)
    total = jnp.sum(prob * grad_prob, axis=1, keepdims=True)
    grad_scores = (prob * (grad_prob - total)).astype(BF)
    dq = join_pair(dot_nn(grad_scores, k)) * SCALE
    dk = dot_tn(grad_scores, split_pair(q)) * SCALE
    dv = dot_tn(prob.astype(BF), g2)
    return dq, dk, dv


def view_backward_kernel(depth, me, z, x, kept, prob_ref, *rest):
    own, others, (out_ref, full_ref, w, sem, full_sem) = rest[:depth], rest[depth : 2 * depth], rest[2 * depth :]
    copies = fetch_weight(me, z, own, others, w, sem)
    out_ref[:, :CW] = kept[:, :CW]
    for copy in copies:
        copy.wait()
    full = pltpu.make_async_copy(w, full_ref, full_sem)
    full.start()
    grad = dot_nt(x[:, 3 * CW : 5 * CW], w[:CW]).astype(BF)
    for j in range(PAIRS):
        at = [slice(i * CW + 128 * j, i * CW + 128 * (j + 1)) for i in range(4)]
        dq, dk, dv = backward_pair(x[:, at[0]], x[:, at[1]], x[:, at[2]], grad[:, at[0]], prob_ref[j])
        out_ref[:, at[1]] = dq.astype(BF)
        out_ref[:, at[2]] = dk.astype(BF)
        out_ref[:, at[3]] = dv.astype(BF)
    full.wait()


def time_backward_kernel(q0, q1, far, near, own, prob_ref, w, dq_ref, own_ref, near_ref, far_ref):
    qct, kv = (q0, q1), (far, near, own)
    rows = PAIR * q0.shape[0]
    grad = dot_nt(rows_of(qct, slice(CW, 3 * CW)), w[...]).astype(BF)
    for j in range(PAIRS):
        at = [slice(i * CW + 128 * j, i * CW + 128 * (j + 1)) for i in range(2)]
        dq, dk, dv = backward_pair(
            rows_of(qct, at[0]), rows_of(kv, at[0]), rows_of(kv, at[1]), grad[:, at[0]], prob_ref[j]
        )
        dq_ref[:, at[0]] = dq.astype(BF)
        for part, value in zip(at, (dk, dv)):
            far_ref[:, part] = value[:rows].astype(BF)
            near_ref[:, part] = value[rows : 2 * rows].astype(BF)
            own_ref[:, part] = value[2 * rows :]


def time_sum_kernel(kept, dq, own, near, far, *outs):
    size = outs[0].shape[0]
    for d, out in enumerate(outs):
        part = slice(d * size, (d + 1) * size)
        out[:, :CW] = kept[part, :CW]
        out[:, CW : 2 * CW] = dq[part]
        out[:, 2 * CW :] = (own[part] + near[part].astype(F32) + far[part].astype(F32)).astype(BF)


def action_kernel(actions, table, out_ref):
    total = None
    for d in range(table.shape[0]):
        codes = iota((actions.shape[0], table.shape[1]), 1)
        one_hot = jnp.where(actions[:, d : d + 1] == codes, 1.0, 0.0).astype(BF)
        term = dot_nn(one_hot, table[d])
        total = term if total is None else total + term
    out_ref[...] = total


def camera_sum_kernel(parts, out_ref, held):
    total = parts[0].astype(F32)
    for i in range(1, parts.shape[0]):
        total = total + parts[i].astype(F32)
    held[...] = total
    size = out_ref.shape[1]
    for i in range(out_ref.shape[0]):
        out_ref[i] = held[i * size : (i + 1) * size, :].astype(BF)


def finish_kernel(me, w, action, t0, t1, view, pred_ref, dq_ref, dk_ref, dv_ref):
    time = (t0, t1)
    rows = view.shape[0]
    frames = rows // 8
    row = iota((rows, rows), 0)
    col = iota((rows, rows), 1)
    source = (((row % 8) // 4) ^ (me[0] % 2)) * 4 * frames + (row // 8) * 4 + row % 4
    perm = jnp.where(col == source, 1.0, 0.0).astype(BF)
    for i, ref in enumerate((dq_ref, dk_ref, dv_ref), 1):
        part = slice(i * CW, (i + 1) * CW)
        ref[:, :CW] = view[:, part]
        ref[:, CW:] = dot_nn(perm, rows_of(time, part)).astype(BF)
    attn_time = dot_nn(perm, rows_of(time, slice(0, CW))).astype(BF)
    mixed = dot_nn(view[:, :CW], w[:CW]) + dot_nn(attn_time, w[CW:])
    total = mixed.reshape(frames, 8, 2 * CW) + action[...][:, None, :]
    pred_ref[...] = total.reshape(rows, 2 * CW).astype(BF)


def whole(shape):
    return pl.BlockSpec(shape, lambda *at: (0,) * len(shape))


def call(kernel, outs, specs, *args, scratch=(), kept=0):
    specs = [whole(arg.shape) if spec is VM else spec for spec, arg in zip(specs, args)]
    count = len(outs) - kept
    return list(
        pl.pallas_call(
            kernel,
            out_shape=[jax.ShapeDtypeStruct(shape, kind) for shape, kind in outs],
            in_specs=specs,
            out_specs=[whole(shape) for shape, _ in outs[:count]] + [ANY] * kept,
            grid=(1,),
            scratch_shapes=list(scratch),
            compiler_params=pltpu.CompilerParams(vmem_limit_bytes=56 * 1024 * 1024),
        )(*args)
    )


def shards(queries, keys, values, cam_valid, windows, actions, act_table, w_out, cotangent):
    _, frames, tokens, width = queries.shape
    rows = frames * tokens
    block = rows // PAIR
    cams = lax.axis_size("cam")
    tm = lax.axis_size("tm")
    at_tm = lax.axis_index("tm")
    core = at_tm % 2
    me = (at_tm % GROUP).reshape(1)
    pair = (at_tm // PAIR).reshape(1)
    group = (at_tm // GROUP).reshape(1)
    depth = tm // GROUP
    same_core = [[2 * i + j for i in range(tm // 2)] for j in range(2)]
    up = [(i, (i + GROUP) % tm) for i in range(tm)]
    down = [(i, (i - GROUP) % tm) for i in range(tm)]
    swap = [(i, i ^ 1) for i in range(tm)]
    beside = [(i, i ^ (tm + 2)) for i in range(cams * tm)]

    w_beside = lax.ppermute(w_out, ("cam", "tm"), beside)
    q, k, v, ct = (a.reshape(rows, width) for a in (queries, keys, values, cotangent))
    packed = call(
        pack_kernel,
        [((rows, 5 * CW + 128), BF)] + [((block, 2 * CW), BF)] * PAIR + [((block, 3 * CW), BF)] * PAIR,
        [SM, SM] + [ANY] * 4,
        me, cam_valid, q, k, v, ct,
        scratch=[pltpu.VMEM((4, rows, width), BF), pltpu.SemaphoreType.DMA((4,))],
    )
    view_send, kv, qct = packed[0], packed[1 : PAIR + 1], packed[PAIR + 1 :]
    w_beside, view_send = lax.optimization_barrier((w_beside, view_send))
    w_both = jnp.concatenate([w_out, w_beside], axis=0)
    view_x = lax.all_to_all(view_send, "cam", 0, 0, tiled=True)
    w_own, w_other = [w_both], []

    def pass_on(first, last):
        for i in range(first, min(last, depth)):
            w_own.append(lax.ppermute(w_own[max(i - 2, 0)], "tm", up if i % 2 else down))

    def swap_blocks(last):
        for block_rows in w_own[len(w_other) : last]:
            w_other.append(lax.ppermute(block_rows, "tm", swap))

    def tie(value):
        value, w_own[:], w_other[:] = lax.optimization_barrier((value, w_own[:], w_other[:]))
        return value

    pass_on(1, 3)
    swap_blocks(1)
    own = jnp.concatenate([kv[0], lax.ppermute(kv[1], "tm", swap)], axis=0)
    near = lax.ppermute(own, "tm", [(i, i + 2) for i in range(tm - 2)])
    far = lax.ppermute(own, "tm", [(i, i + 4) for i in range(tm - 4)])
    q0, q1 = qct[0], lax.ppermute(qct[1], "tm", swap)

    q0 = tie(q0)
    pass_on(3, 5)
    swap_blocks(3)
    (action_sum,) = call(action_kernel, [((frames, width), F32)], [VM] * 2, actions, act_table)
    view_x, action_sum = lax.optimization_barrier((view_x, action_sum))
    near, far = tie((near, far))
    pass_on(5, 7)
    swap_blocks(5)
    kept_view, view_swap, prob_view = call(
        view_forward_kernel,
        [((rows, 2 * CW), BF)] * 2 + [((PAIRS, 2 * rows, rows), F32)],
        [SM, VM],
        me, view_x,
    )
    kept_time, time_swap, prob_time = call(
        time_forward_kernel,
        [((rows, 2 * CW), BF)] * 2 + [((PAIRS, 2 * rows, 3 * rows), F32)],
        [SM] * 3 + [VM] * 5,
        windows, me, pair, q0, q1, far, near, own,
    )

    kept_view = tie(kept_view)
    pass_on(7, depth)
    swap_blocks(depth)
    view_swap = lax.ppermute(view_swap, "tm", swap)
    time_swap = lax.ppermute(time_swap, "tm", swap)
    grad_norm = 1.0 / math.sqrt(cams * tm * rows)
    (part,) = call(
        functools.partial(weight_kernel, grad_norm),
        [((width, CW), BF)],
        [VM] * 4,
        kept_view, view_swap, kept_time, time_swap,
    )
    part = lax.all_to_all(part.reshape(cams, width // cams, CW), "cam", 0, 0, tiled=True)

    view_out, w_full = call(
        functools.partial(view_backward_kernel, depth),
        [((rows, 4 * CW), BF), ((width, width), BF)],
        [SM] * 2 + [VM] * 3 + [ANY] * (2 * depth),
        me, group, view_x, kept_view, prob_view, *w_own, *w_other,
        scratch=[pltpu.VMEM((width, width), BF), pltpu.SemaphoreType.DMA((tm,)), pltpu.SemaphoreType.DMA],
        kept=1,
    )
    q0, view_out = lax.optimization_barrier((q0, view_out))
    view_back = lax.all_to_all(view_out, "cam", 0, 0, tiled=True)
    dq_time, own_grad, near_grad, far_grad = call(
        time_backward_kernel,
        [((rows, CW), BF), ((rows, 2 * CW), F32), ((rows, 2 * CW), BF), ((rows, 2 * CW), BF)],
        [VM] * 6 + [pl.BlockSpec((CW, width), lambda *at: (1, 0))],
        q0, q1, far, near, own, prob_time, w_full,
    )
    part, near_grad = lax.optimization_barrier((part, near_grad))
    near_grad = lax.ppermute(near_grad, "tm", [(i + 2, i) for i in range(tm - 2)])
    far_grad = lax.ppermute(far_grad, "tm", [(i + 4, i) for i in range(tm - 4)])

    chips = tm // 2
    (part,) = call(
        camera_sum_kernel,
        [((chips, width // cams // chips, CW), BF)],
        [VM],
        part,
        scratch=[pltpu.VMEM((width // cams, CW), F32)],
    )
    part, view_back, near_grad, far_grad = lax.optimization_barrier((part, view_back, near_grad, far_grad))
    part = lax.all_to_all(part, "tm", 0, 0, tiled=True, axis_index_groups=same_core)
    part = jnp.sum(part.astype(F32), axis=0)
    final = width // cams // tm
    mine = lax.dynamic_slice_in_dim(part, core * final, final, 0)
    theirs = lax.ppermute(lax.dynamic_slice_in_dim(part, (1 - core) * final, final, 0), "tm", swap)
    grad_out_weight = jnp.concatenate(
        [jnp.where(core == 0, mine, theirs), jnp.where(core == 0, theirs, mine)], axis=1
    )

    t0, t1 = call(
        time_sum_kernel, [((block, 4 * CW), BF)] * PAIR, [VM] * 5, kept_time, dq_time, own_grad, near_grad, far_grad
    )
    t1 = lax.ppermute(t1, "tm", swap)
    outs = call(
        finish_kernel,
        [((rows, width), BF)] * 4,
        [SM] + [VM] * 5,
        me, w_full, action_sum, t0, t1, view_back,
    )
    return tuple(a.reshape(1, frames, tokens, width) for a in outs) + (grad_out_weight,)


def solution(mesh):
    in_specs = (
        P("cam", "tm", None, None),
        P("cam", "tm", None, None),
        P("cam", "tm", None, None),
        P("cam", "tm"),
        P(),
        P("tm", None),
        P(),
        P("tm", None),
        P("cam", "tm", None, None),
    )
    out_specs = (
        P("cam", "tm", None, None),
        P("cam", "tm", None, None),
        P("cam", "tm", None, None),
        P("cam", "tm", None, None),
        P(("cam", "tm"), None),
    )
    return jax.shard_map(shards, mesh=mesh, in_specs=in_specs, out_specs=out_specs, check_vma=False)
```

```python
import functools
import math

import jax
import jax.numpy as jnp
from jax import lax
from jax.experimental import pallas as pl
from jax.experimental.pallas import tpu as pltpu
from jax.sharding import PartitionSpec as P

HC = 12
HT = 12
HD = 64
WIN = 64
CW = HC * HD
GROUP = 4
PAIR = 2
SCALE = HD ** (-0.5)
BF = jnp.bfloat16
F32 = jnp.float32
PAIRS = HC // 2
VM = pl.BlockSpec(memory_space=pltpu.VMEM)
ANY = pl.BlockSpec(memory_space=pl.ANY)
SM = pl.BlockSpec(memory_space=pltpu.SMEM)


def iota(shape, dim):
    return lax.broadcasted_iota(jnp.int32, shape, dim)


def dot_nt(a, b):
    return lax.dot_general(a, b, (((1,), (1,)), ((), ())), preferred_element_type=F32)


def dot_tn(a, b):
    return lax.dot_general(a, b, (((0,), (0,)), ((), ())), preferred_element_type=F32)


def dot_nn(a, b):
    return jnp.dot(a, b, preferred_element_type=F32)


def split_pair(rows):
    low = iota(rows.shape, 1) < HD
    zero = jnp.zeros_like(rows)
    return jnp.concatenate([jnp.where(low, rows, zero), jnp.where(low, zero, rows)], axis=0)


def join_pair(rows):
    count = rows.shape[0] // 2
    low = iota((count, rows.shape[1]), 1) < HD
    return jnp.where(low, rows[:count], rows[count:])


def softmax_pair(q, k, mask):
    scores = dot_nt(split_pair(q), k) * SCALE
    scores = jnp.where(mask, scores, -jnp.inf)
    largest = jnp.max(scores, axis=1, keepdims=True)
    e = jnp.exp(scores - largest)
    return e / jnp.sum(e, axis=1, keepdims=True)


def pack_kernel(me, valid, q, k, v, ct, view_ref, *rest):
    kv_refs, qct_refs, (held, sems) = rest[:PAIR], rest[PAIR : 2 * PAIR], rest[2 * PAIR :]
    copies = [pltpu.make_async_copy(ref, held.at[i], sems.at[i]) for i, ref in enumerate((q, k, v, ct))]
    for copy in copies:
        copy.start()
    rows = q.shape[0]
    frames = rows // 8
    block = 4 * frames
    row = iota((rows, rows), 0)
    col = iota((rows, rows), 1)
    source = ((row // 4) % frames) * 8 + 4 * ((row // block) ^ (me[0] % 2)) + row % 4
    perm = jnp.where(col == source, 1.0, 0.0).astype(BF)
    frame = iota((rows, 128), 0) // 8
    flags = jnp.zeros((rows, 128), F32)
    for f in range(frames):
        flags = jnp.where(frame == f, valid[0, f].astype(F32), flags)
    view_ref[:, 5 * CW :] = jnp.where(flags > 0.5, 1.0, 0.0).astype(BF)
    for i in range(4):
        copies[i].wait()
        if i < 3:
            view_ref[:, i * CW : (i + 1) * CW] = held[i, :, :CW]
            moved = dot_nn(perm, held[i, :, CW:]).astype(BF)
        else:
            view_ref[:, 3 * CW : 5 * CW] = held[i]
            moved = dot_nn(perm, held[i]).astype(BF)
        for d in range(PAIR):
            part = moved[d * block : (d + 1) * block]
            if i in (1, 2):
                kv_refs[d][:, (i - 1) * CW : i * CW] = part
            elif i == 0:
                qct_refs[d][:, :CW] = part
            else:
                qct_refs[d][:, CW:] = part


def view_mask(flags):
    rows = flags.shape[0]
    pick = jnp.where(iota((8, 128), 1) == 0, 1.0, 0.0).astype(BF)
    valid_row = dot_nt(pick, flags)[:1]
    r = iota((2 * rows, rows), 0) % rows
    c = iota((2 * rows, rows), 1)
    same_frame = ((r // 8) % 2) == ((c // 8) % 2)
    return same_frame & ((valid_row > 0.5) | (r // 16 == c // 16))


def keep_for_weight(attn, ct, core, own_ref, send_ref):
    own_ref[:, :CW] = attn
    send_ref[:, :CW] = attn
    own_ref[:, CW:] = jnp.where(core == 0, ct[:, :CW], ct[:, CW:])
    send_ref[:, CW:] = jnp.where(core == 0, ct[:, CW:], ct[:, :CW])


def view_forward_kernel(me, x, own_ref, send_ref, prob_ref):
    mask = view_mask(x[:, 5 * CW :])
    attn = []
    for j in range(PAIRS):
        q = x[:, 128 * j : 128 * (j + 1)]
        k = x[:, CW + 128 * j : CW + 128 * (j + 1)]
        v = x[:, 2 * CW + 128 * j : 2 * CW + 128 * (j + 1)]
        prob = softmax_pair(q, k, mask)
        prob_ref[j] = prob
        attn.append(join_pair(dot_nn(prob.astype(BF), v)).astype(BF))
    keep_for_weight(jnp.concatenate(attn, axis=1), x[:, 3 * CW : 5 * CW], me[0] % 2, own_ref, send_ref)


def rows_of(refs, columns):
    return jnp.concatenate([ref[:, columns] for ref in refs], axis=0)


def time_forward_kernel(windows, me, pair, q0, q1, far, near, own, own_ref, send_ref, prob_ref):
    qct, kv = (q0, q1), (far, near, own)
    size = q0.shape[0]
    rows = PAIR * size
    shape = (2 * rows, 3 * rows)
    r = iota(shape, 0)
    c = iota(shape, 1)
    second = r >= rows
    core = me[0] % 2
    span = size // 2

    def frame_of(row):
        return ((row // size) ^ core) * (size // 4) + (row % size) // 4

    key_frame = frame_of(c % rows) + span * (c // rows) - 2 * span
    gap = frame_of(r % rows) - key_frame
    base = (r % 4 == c % 4) & (gap >= 0) & (key_frame + span * pair[0] >= 0)
    attn = []
    for j in range(PAIRS):
        at = [slice(i * CW + 128 * j, i * CW + 128 * (j + 1)) for i in range(2)]
        limit = jnp.where(second, windows[2 * j + 1], windows[2 * j])
        prob = softmax_pair(rows_of(qct, at[0]), rows_of(kv, at[0]), base & (gap < limit))
        prob_ref[j] = prob
        attn.append(join_pair(dot_nn(prob.astype(BF), rows_of(kv, at[1]))).astype(BF))
    keep_for_weight(jnp.concatenate(attn, axis=1), rows_of(qct, slice(CW, 3 * CW)), core, own_ref, send_ref)


def weight_kernel(scale, own_view, other_view, own_time, other_time, out_ref):
    for i, (own, other) in enumerate(((own_view, other_view), (own_time, other_time))):
        left = jnp.concatenate([own[:, :CW], other[:, :CW]], axis=0)
        right = jnp.concatenate([own[:, CW:], other[:, CW:]], axis=0)
        out_ref[i * CW : (i + 1) * CW, :] = (dot_tn(left, right) * scale).astype(BF)


def fetch_weight(me, z, own, others, held, sem):
    depth = len(own)
    size = own[0].shape[0] // 2
    core, y = me[0] % 2, me[0] // 2
    copies = []
    for i in range(depth):
        place = lax.rem(z[0] + offset(i, depth), depth)
        for n, (which, ref) in enumerate(((core, own[i]), (1 - core, others[i]))):
            for e in range(2):
                start = pl.multiple_of((4 * place + 2 * (y ^ e) + which) * size, 16)
                copies.append(
                    pltpu.make_async_copy(
                        ref.at[pl.ds(e * size, size)], held.at[pl.ds(start, size)], sem.at[4 * i + 2 * n + e]
                    )
                )
    for copy in copies:
        copy.start()
    return copies


def offset(i, depth):
    return (i + 1) // 2 if i % 2 == 0 else depth - (i + 1) // 2


def backward_pair(q, k, v, g, prob):
    g2 = split_pair(g)
    grad_prob = dot_nt(g2, v)
    total = jnp.sum(prob * grad_prob, axis=1, keepdims=True)
    grad_scores = (prob * (grad_prob - total)).astype(BF)
    dq = join_pair(dot_nn(grad_scores, k)) * SCALE
    dk = dot_tn(grad_scores, split_pair(q)) * SCALE
    dv = dot_tn(prob.astype(BF), g2)
    return dq, dk, dv


def time_backward_kernel(depth, me, z, q0, q1, far, near, own, prob_ref, *rest):
    w_own, w_other, rest = rest[:depth], rest[depth : 2 * depth], rest[2 * depth :]
    dq_ref, own_ref, near_ref, far_ref, full_ref, w, sem, full_sem = rest
    copies = fetch_weight(me, z, w_own, w_other, w, sem)
    qct, kv = (q0, q1), (far, near, own)
    rows = PAIR * q0.shape[0]
    for copy in copies:
        copy.wait()
    full = pltpu.make_async_copy(w, full_ref, full_sem)
    full.start()
    grad = dot_nt(rows_of(qct, slice(CW, 3 * CW)), w[CW:]).astype(BF)
    for j in range(PAIRS):
        at = [slice(i * CW + 128 * j, i * CW + 128 * (j + 1)) for i in range(2)]
        dq, dk, dv = backward_pair(
            rows_of(qct, at[0]), rows_of(kv, at[0]), rows_of(kv, at[1]), grad[:, at[0]], prob_ref[j]
        )
        dq_ref[:, at[0]] = dq.astype(BF)
        for part, value in zip(at, (dk, dv)):
            far_ref[:, part] = value[:rows].astype(BF)
            near_ref[:, part] = value[rows : 2 * rows].astype(BF)
            own_ref[:, part] = value[2 * rows :]
    full.wait()


def view_backward_kernel(cam, x, kept, prob_ref, w, *rest):
    out_refs, held = rest[:-1], rest[-1]
    held[:, :CW] = kept[:, :CW]
    grad = dot_nt(x[:, 3 * CW : 5 * CW], w[...]).astype(BF)
    for j in range(PAIRS):
        at = [slice(i * CW + 128 * j, i * CW + 128 * (j + 1)) for i in range(4)]
        dq, dk, dv = backward_pair(x[:, at[0]], x[:, at[1]], x[:, at[2]], grad[:, at[0]], prob_ref[j])
        held[:, at[1]] = dq.astype(BF)
        held[:, at[2]] = dk.astype(BF)
        held[:, at[3]] = dv.astype(BF)
    size = held.shape[0] // len(out_refs)
    for d, out in enumerate(out_refs):
        out[...] = held[pl.ds(pl.multiple_of((cam[0] ^ d) * size, size), size), :]


def time_sum_kernel(kept, dq, own, near, far, *outs):
    size = outs[0].shape[0]
    for d, out in enumerate(outs):
        part = slice(d * size, (d + 1) * size)
        out[:, :CW] = kept[part, :CW]
        out[:, CW : 2 * CW] = dq[part]
        out[:, 2 * CW :] = (own[part] + near[part].astype(F32) + far[part].astype(F32)).astype(BF)


def action_kernel(actions, table, out_ref):
    total = None
    for d in range(table.shape[0]):
        codes = iota((actions.shape[0], table.shape[1]), 1)
        one_hot = jnp.where(actions[:, d : d + 1] == codes, 1.0, 0.0).astype(BF)
        term = dot_nn(one_hot, table[d])
        total = term if total is None else total + term
    out_ref[...] = total


def camera_sum_kernel(parts, out_ref, held):
    total = parts[0].astype(F32)
    for i in range(1, parts.shape[0]):
        total = total + parts[i].astype(F32)
    held[...] = total
    size = out_ref.shape[1]
    for i in range(out_ref.shape[0]):
        out_ref[i] = held[i * size : (i + 1) * size, :].astype(BF)


def finish_kernel(cams, me, cam, w, action, t0, t1, *rest):
    blocks, (pred_ref, dq_ref, dk_ref, dv_ref, view) = rest[:cams], rest[cams:]
    time = (t0, t1)
    share = blocks[0].shape[0]
    for d, part in enumerate(blocks):
        view[pl.ds(pl.multiple_of((cam[0] ^ d) * share, share), share), :] = part[...]
    rows = view.shape[0]
    frames = rows // 8
    row = iota((rows, rows), 0)
    col = iota((rows, rows), 1)
    source = (((row % 8) // 4) ^ (me[0] % 2)) * 4 * frames + (row // 8) * 4 + row % 4
    perm = jnp.where(col == source, 1.0, 0.0).astype(BF)
    for i, ref in enumerate((dq_ref, dk_ref, dv_ref), 1):
        part = slice(i * CW, (i + 1) * CW)
        ref[:, :CW] = view[:, part]
        ref[:, CW:] = dot_nn(perm, rows_of(time, part)).astype(BF)
    attn_time = dot_nn(perm, rows_of(time, slice(0, CW))).astype(BF)
    mixed = dot_nn(view[:, :CW], w[:CW]) + dot_nn(attn_time, w[CW:])
    total = mixed.reshape(frames, 8, 2 * CW) + action[...][:, None, :]
    pred_ref[...] = total.reshape(rows, 2 * CW).astype(BF)


def whole(shape):
    return pl.BlockSpec(shape, lambda *at: (0,) * len(shape))


def call(kernel, outs, specs, *args, scratch=(), kept=0):
    specs = [whole(arg.shape) if spec is VM else spec for spec, arg in zip(specs, args)]
    count = len(outs) - kept
    return list(
        pl.pallas_call(
            kernel,
            out_shape=[jax.ShapeDtypeStruct(shape, kind) for shape, kind in outs],
            in_specs=specs,
            out_specs=[whole(shape) for shape, _ in outs[:count]] + [ANY] * kept,
            grid=(1,),
            scratch_shapes=list(scratch),
            compiler_params=pltpu.CompilerParams(vmem_limit_bytes=56 * 1024 * 1024),
        )(*args)
    )


def shards(queries, keys, values, cam_valid, windows, actions, act_table, w_out, cotangent):
    _, frames, tokens, width = queries.shape
    rows = frames * tokens
    block = rows // PAIR
    cams = lax.axis_size("cam")
    tm = lax.axis_size("tm")
    at_tm = lax.axis_index("tm")
    core = at_tm % 2
    me = (at_tm % GROUP).reshape(1)
    pair = (at_tm // PAIR).reshape(1)
    group = (at_tm // GROUP).reshape(1)
    depth = tm // GROUP
    same_core = [[2 * i + j for i in range(tm // 2)] for j in range(2)]
    up = [(i, (i + GROUP) % tm) for i in range(tm)]
    down = [(i, (i - GROUP) % tm) for i in range(tm)]
    swap = [(i, i ^ 1) for i in range(tm)]
    beside = [(i, i ^ (tm + 2)) for i in range(cams * tm)]

    w_beside = lax.ppermute(w_out, ("cam", "tm"), beside)
    q, k, v, ct = (a.reshape(rows, width) for a in (queries, keys, values, cotangent))
    packed = call(
        pack_kernel,
        [((rows, 5 * CW + 128), BF)] + [((block, 2 * CW), BF)] * PAIR + [((block, 3 * CW), BF)] * PAIR,
        [SM, SM] + [ANY] * 4,
        me, cam_valid, q, k, v, ct,
        scratch=[pltpu.VMEM((4, rows, width), BF), pltpu.SemaphoreType.DMA((4,))],
    )
    view_send, kv, qct = packed[0], packed[1 : PAIR + 1], packed[PAIR + 1 :]
    w_beside, view_send = lax.optimization_barrier((w_beside, view_send))
    w_both = jnp.concatenate([w_out, w_beside], axis=0)
    view_x = lax.all_to_all(view_send, "cam", 0, 0, tiled=True)
    w_own, w_other = [w_both], []

    def pass_on(first, last):
        for i in range(first, min(last, depth)):
            w_own.append(lax.ppermute(w_own[max(i - 2, 0)], "tm", up if i % 2 else down))

    def swap_blocks(last):
        for block_rows in w_own[len(w_other) : last]:
            w_other.append(lax.ppermute(block_rows, "tm", swap))

    def tie(value):
        value, w_own[:], w_other[:] = lax.optimization_barrier((value, w_own[:], w_other[:]))
        return value

    own = jnp.concatenate([kv[0], lax.ppermute(kv[1], "tm", swap)], axis=0)
    q0, q1 = qct[0], lax.ppermute(qct[1], "tm", swap)

    own = tie(own)
    near = lax.ppermute(own, "tm", [(i, i + 2) for i in range(tm - 2)])
    far = lax.ppermute(own, "tm", [(i, i + 4) for i in range(tm - 4)])
    pass_on(1, 3)
    (action_sum,) = call(action_kernel, [((frames, width), F32)], [VM] * 2, actions, act_table)
    near, far = tie((near, far))
    pass_on(3, 5)
    swap_blocks(1)
    view_x = tie(view_x)
    pass_on(5, 7)
    swap_blocks(5)
    kept_view, view_swap, prob_view = call(
        view_forward_kernel,
        [((rows, 2 * CW), BF)] * 2 + [((PAIRS, 2 * rows, rows), F32)],
        [SM, VM],
        me, view_x,
    )
    kept_time, time_swap, prob_time = call(
        time_forward_kernel,
        [((rows, 2 * CW), BF)] * 2 + [((PAIRS, 2 * rows, 3 * rows), F32)],
        [SM] * 3 + [VM] * 5,
        windows, me, pair, q0, q1, far, near, own,
    )

    pass_on(7, depth)
    swap_blocks(depth)
    view_swap = lax.ppermute(view_swap, "tm", swap)
    time_swap = lax.ppermute(time_swap, "tm", swap)
    grad_norm = 1.0 / math.sqrt(cams * tm * rows)
    (part,) = call(
        functools.partial(weight_kernel, grad_norm),
        [((width, CW), BF)],
        [VM] * 4,
        kept_view, view_swap, kept_time, time_swap,
    )
    part = lax.all_to_all(part.reshape(cams, width // cams, CW), "cam", 0, 0, tiled=True)

    q0, action_sum = lax.optimization_barrier((q0, action_sum))
    dq_time, own_grad, near_grad, far_grad, w_full = call(
        functools.partial(time_backward_kernel, depth),
        [((rows, CW), BF), ((rows, 2 * CW), F32)] + [((rows, 2 * CW), BF)] * 2 + [((width, width), BF)],
        [SM] * 2 + [VM] * 6 + [ANY] * (2 * depth),
        me, group, q0, q1, far, near, own, prob_time, *w_own, *w_other,
        scratch=[pltpu.VMEM((width, width), BF), pltpu.SemaphoreType.DMA((tm,)), pltpu.SemaphoreType.DMA],
        kept=1,
    )
    view_x, near_grad = lax.optimization_barrier((view_x, near_grad))
    near_grad = lax.ppermute(near_grad, "tm", [(i + 2, i) for i in range(tm - 2)])
    far_grad = lax.ppermute(far_grad, "tm", [(i + 4, i) for i in range(tm - 4)])
    cam = lax.axis_index("cam").reshape(1)
    view_out = call(
        view_backward_kernel,
        [((rows // cams, 4 * CW), BF)] * cams,
        [SM] + [VM] * 3 + [pl.BlockSpec((CW, width), lambda *at: (0, 0))],
        cam, view_x, kept_view, prob_view, w_full,
        scratch=[pltpu.VMEM((rows, 4 * CW), BF)],
    )
    view_back = [view_out[0]] + [
        lax.ppermute(view_out[d], "cam", [(i, i ^ d) for i in range(cams)]) for d in range(1, cams)
    ]
    part, near_grad, far_grad, view_back[1] = lax.optimization_barrier((part, near_grad, far_grad, view_back[1]))

    chips = tm // 2
    (part,) = call(
        camera_sum_kernel,
        [((chips, width // cams // chips, CW), BF)],
        [VM],
        part,
        scratch=[pltpu.VMEM((width // cams, CW), F32)],
    )
    part = lax.all_to_all(part, "tm", 0, 0, tiled=True, axis_index_groups=same_core)
    part = jnp.sum(part.astype(F32), axis=0)
    final = width // cams // tm
    mine = lax.dynamic_slice_in_dim(part, core * final, final, 0)
    theirs = lax.ppermute(lax.dynamic_slice_in_dim(part, (1 - core) * final, final, 0), "tm", swap)
    grad_out_weight = jnp.concatenate(
        [jnp.where(core == 0, mine, theirs), jnp.where(core == 0, theirs, mine)], axis=1
    )

    t0, t1 = call(
        time_sum_kernel, [((block, 4 * CW), BF)] * PAIR, [VM] * 5, kept_time, dq_time, own_grad, near_grad, far_grad
    )
    t1 = lax.ppermute(t1, "tm", swap)
    outs = call(
        functools.partial(finish_kernel, cams),
        [((rows, width), BF)] * 4,
        [SM] * 2 + [VM] * (4 + cams),
        me, cam, w_full, action_sum, t0, t1, *view_back,
        scratch=[pltpu.VMEM((rows, 4 * CW), BF)],
    )
    return tuple(a.reshape(1, frames, tokens, width) for a in outs) + (grad_out_weight,)


def solution(mesh):
    in_specs = (
        P("cam", "tm", None, None),
        P("cam", "tm", None, None),
        P("cam", "tm", None, None),
        P("cam", "tm"),
        P(),
        P("tm", None),
        P(),
        P("tm", None),
        P("cam", "tm", None, None),
    )
    out_specs = (
        P("cam", "tm", None, None),
        P("cam", "tm", None, None),
        P("cam", "tm", None, None),
        P("cam", "tm", None, None),
        P(("cam", "tm"), None),
    )
    return jax.shard_map(shards, mesh=mesh, in_specs=in_specs, out_specs=out_specs, check_vma=False)
```

```python
import functools
import math

import jax
import jax.numpy as jnp
from jax import lax
from jax.experimental import pallas as pl
from jax.experimental.pallas import tpu as pltpu
from jax.sharding import PartitionSpec as P

HC = 12
HT = 12
HD = 64
WIN = 64
CW = HC * HD
GROUP = 4
PAIR = 2
SCALE = HD ** (-0.5)
BF = jnp.bfloat16
F32 = jnp.float32
PAIRS = HC // 2
VM = pl.BlockSpec(memory_space=pltpu.VMEM)
ANY = pl.BlockSpec(memory_space=pl.ANY)
SM = pl.BlockSpec(memory_space=pltpu.SMEM)


def iota(shape, dim):
    return lax.broadcasted_iota(jnp.int32, shape, dim)


def dot_nt(a, b):
    return lax.dot_general(a, b, (((1,), (1,)), ((), ())), preferred_element_type=F32)


def dot_tn(a, b):
    return lax.dot_general(a, b, (((0,), (0,)), ((), ())), preferred_element_type=F32)


def dot_nn(a, b):
    return jnp.dot(a, b, preferred_element_type=F32)


def split_pair(rows):
    low = iota(rows.shape, 1) < HD
    zero = jnp.zeros_like(rows)
    return jnp.concatenate([jnp.where(low, rows, zero), jnp.where(low, zero, rows)], axis=0)


def join_pair(rows):
    count = rows.shape[0] // 2
    low = iota((count, rows.shape[1]), 1) < HD
    return jnp.where(low, rows[:count], rows[count:])


def softmax_pair(q, k, mask):
    scores = dot_nt(split_pair(q), k) * SCALE
    scores = jnp.where(mask, scores, -jnp.inf)
    largest = jnp.max(scores, axis=1, keepdims=True)
    e = jnp.exp(scores - largest)
    return e / jnp.sum(e, axis=1, keepdims=True)


def pack_kernel(me, valid, q, k, v, ct, view_ref, *rest):
    kv_refs, qct_refs, (held, sems) = rest[:PAIR], rest[PAIR : 2 * PAIR], rest[2 * PAIR :]
    copies = [pltpu.make_async_copy(ref, held.at[i], sems.at[i]) for i, ref in enumerate((q, k, v, ct))]
    for copy in copies:
        copy.start()
    rows = q.shape[0]
    frames = rows // 8
    block = 4 * frames
    row = iota((rows, rows), 0)
    col = iota((rows, rows), 1)
    source = ((row // 4) % frames) * 8 + 4 * ((row // block) ^ (me[0] % 2)) + row % 4
    perm = jnp.where(col == source, 1.0, 0.0).astype(BF)
    frame = iota((rows, 128), 0) // 8
    flags = jnp.zeros((rows, 128), F32)
    for f in range(frames):
        flags = jnp.where(frame == f, valid[0, f].astype(F32), flags)
    view_ref[:, 5 * CW :] = jnp.where(flags > 0.5, 1.0, 0.0).astype(BF)
    for i in range(4):
        copies[i].wait()
        if i < 3:
            view_ref[:, i * CW : (i + 1) * CW] = held[i, :, :CW]
            moved = dot_nn(perm, held[i, :, CW:]).astype(BF)
        else:
            view_ref[:, 3 * CW : 5 * CW] = held[i]
            moved = dot_nn(perm, held[i]).astype(BF)
        for d in range(PAIR):
            part = moved[d * block : (d + 1) * block]
            if i in (1, 2):
                kv_refs[d][:, (i - 1) * CW : i * CW] = part
            elif i == 0:
                qct_refs[d][:, :CW] = part
            else:
                qct_refs[d][:, CW:] = part


def view_mask(flags):
    rows = flags.shape[0]
    pick = jnp.where(iota((8, 128), 1) == 0, 1.0, 0.0).astype(BF)
    valid_row = dot_nt(pick, flags)[:1]
    r = iota((2 * rows, rows), 0) % rows
    c = iota((2 * rows, rows), 1)
    same_frame = ((r // 8) % 2) == ((c // 8) % 2)
    return same_frame & ((valid_row > 0.5) | (r // 16 == c // 16))


def keep_for_weight(attn, ct, core, own_ref, send_ref):
    own_ref[:, :CW] = attn
    send_ref[:, :CW] = attn
    own_ref[:, CW:] = jnp.where(core == 0, ct[:, :CW], ct[:, CW:])
    send_ref[:, CW:] = jnp.where(core == 0, ct[:, CW:], ct[:, :CW])


def view_forward_kernel(me, x, own_ref, send_ref, prob_ref):
    mask = view_mask(x[:, 5 * CW :])
    attn = []
    for j in range(PAIRS):
        q = x[:, 128 * j : 128 * (j + 1)]
        k = x[:, CW + 128 * j : CW + 128 * (j + 1)]
        v = x[:, 2 * CW + 128 * j : 2 * CW + 128 * (j + 1)]
        prob = softmax_pair(q, k, mask)
        prob_ref[j] = prob
        attn.append(join_pair(dot_nn(prob.astype(BF), v)).astype(BF))
    keep_for_weight(jnp.concatenate(attn, axis=1), x[:, 3 * CW : 5 * CW], me[0] % 2, own_ref, send_ref)


def rows_of(refs, columns):
    return jnp.concatenate([ref[:, columns] for ref in refs], axis=0)


def time_forward_kernel(windows, me, pair, q0, q1, far, near, own, own_ref, send_ref, prob_ref):
    qct, kv = (q0, q1), (far, near, own)
    size = q0.shape[0]
    rows = PAIR * size
    shape = (2 * rows, 3 * rows)
    r = iota(shape, 0)
    c = iota(shape, 1)
    second = r >= rows
    core = me[0] % 2
    span = size // 2

    def frame_of(row):
        return ((row // size) ^ core) * (size // 4) + (row % size) // 4

    key_frame = frame_of(c % rows) + span * (c // rows) - 2 * span
    gap = frame_of(r % rows) - key_frame
    base = (r % 4 == c % 4) & (gap >= 0) & (key_frame + span * pair[0] >= 0)
    attn = []
    for j in range(PAIRS):
        at = [slice(i * CW + 128 * j, i * CW + 128 * (j + 1)) for i in range(2)]
        limit = jnp.where(second, windows[2 * j + 1], windows[2 * j])
        prob = softmax_pair(rows_of(qct, at[0]), rows_of(kv, at[0]), base & (gap < limit))
        prob_ref[j] = prob
        attn.append(join_pair(dot_nn(prob.astype(BF), rows_of(kv, at[1]))).astype(BF))
    keep_for_weight(jnp.concatenate(attn, axis=1), rows_of(qct, slice(CW, 3 * CW)), core, own_ref, send_ref)


def weight_kernel(scale, own_view, other_view, own_time, other_time, out_ref):
    for i, (own, other) in enumerate(((own_view, other_view), (own_time, other_time))):
        left = jnp.concatenate([own[:, :CW], other[:, :CW]], axis=0)
        right = jnp.concatenate([own[:, CW:], other[:, CW:]], axis=0)
        out_ref[i * CW : (i + 1) * CW, :] = (dot_tn(left, right) * scale).astype(BF)


def fetch_weight(me, z, own, others, held, sem):
    depth = len(own)
    size = own[0].shape[0] // 2
    core, y = me[0] % 2, me[0] // 2
    copies = []
    for i in range(depth):
        place = lax.rem(z[0] + offset(i, depth), depth)
        for n, (which, ref) in enumerate(((core, own[i]), (1 - core, others[i]))):
            for e in range(2):
                start = pl.multiple_of((4 * place + 2 * (y ^ e) + which) * size, 16)
                copies.append(
                    pltpu.make_async_copy(
                        ref.at[pl.ds(e * size, size)], held.at[pl.ds(start, size)], sem.at[4 * i + 2 * n + e]
                    )
                )
    for copy in copies:
        copy.start()
    return copies


def offset(i, depth):
    return (i + 1) // 2 if i % 2 == 0 else depth - (i + 1) // 2


def backward_pair(q, k, v, g, prob):
    g2 = split_pair(g)
    grad_prob = dot_nt(g2, v)
    total = jnp.sum(prob * grad_prob, axis=1, keepdims=True)
    grad_scores = (prob * (grad_prob - total)).astype(BF)
    dq = join_pair(dot_nn(grad_scores, k)) * SCALE
    dk = dot_tn(grad_scores, split_pair(q)) * SCALE
    dv = dot_tn(prob.astype(BF), g2)
    return dq, dk, dv


def time_backward_kernel(depth, me, z, q0, q1, far, near, own, prob_ref, *rest):
    w_own, w_other, rest = rest[:depth], rest[depth : 2 * depth], rest[2 * depth :]
    dq_ref, own_ref, near_ref, far_ref, full_ref, w, sem, full_sem = rest
    copies = fetch_weight(me, z, w_own, w_other, w, sem)
    qct, kv = (q0, q1), (far, near, own)
    rows = PAIR * q0.shape[0]
    for copy in copies:
        copy.wait()
    full = pltpu.make_async_copy(w, full_ref, full_sem)
    full.start()
    grad = dot_nt(rows_of(qct, slice(CW, 3 * CW)), w[CW:]).astype(BF)
    for j in range(PAIRS):
        at = [slice(i * CW + 128 * j, i * CW + 128 * (j + 1)) for i in range(2)]
        dq, dk, dv = backward_pair(
            rows_of(qct, at[0]), rows_of(kv, at[0]), rows_of(kv, at[1]), grad[:, at[0]], prob_ref[j]
        )
        dq_ref[:, at[0]] = dq.astype(BF)
        for part, value in zip(at, (dk, dv)):
            far_ref[:, part] = value[:rows].astype(BF)
            near_ref[:, part] = value[rows : 2 * rows].astype(BF)
            own_ref[:, part] = value[2 * rows :]
    full.wait()


def view_backward_kernel(cam, x, kept, prob_ref, w, *rest):
    out_refs, held = rest[:-1], rest[-1]
    held[:, :CW] = kept[:, :CW]
    grad = dot_nt(x[:, 3 * CW : 5 * CW], w[...]).astype(BF)
    for j in range(PAIRS):
        at = [slice(i * CW + 128 * j, i * CW + 128 * (j + 1)) for i in range(4)]
        dq, dk, dv = backward_pair(x[:, at[0]], x[:, at[1]], x[:, at[2]], grad[:, at[0]], prob_ref[j])
        held[:, at[1]] = dq.astype(BF)
        held[:, at[2]] = dk.astype(BF)
        held[:, at[3]] = dv.astype(BF)
    size = held.shape[0] // len(out_refs)
    for d, out in enumerate(out_refs):
        out[...] = held[pl.ds(pl.multiple_of((cam[0] ^ d) * size, size), size), :]


def time_sum_kernel(kept, dq, own, near, far, *outs):
    size = outs[0].shape[0]
    for d, out in enumerate(outs):
        part = slice(d * size, (d + 1) * size)
        out[:, :CW] = kept[part, :CW]
        out[:, CW : 2 * CW] = dq[part]
        out[:, 2 * CW :] = (own[part] + near[part].astype(F32) + far[part].astype(F32)).astype(BF)


def action_kernel(actions, table, out_ref):
    total = None
    for d in range(table.shape[0]):
        codes = iota((actions.shape[0], table.shape[1]), 1)
        one_hot = jnp.where(actions[:, d : d + 1] == codes, 1.0, 0.0).astype(BF)
        term = dot_nn(one_hot, table[d])
        total = term if total is None else total + term
    out_ref[...] = total


def camera_sum_kernel(parts, out_ref, held):
    total = parts[0].astype(F32)
    for i in range(1, parts.shape[0]):
        total = total + parts[i].astype(F32)
    held[...] = total
    size = out_ref.shape[1]
    for i in range(out_ref.shape[0]):
        out_ref[i] = held[i * size : (i + 1) * size, :].astype(BF)


def finish_kernel(cams, me, cam, w, action, t0, t1, *rest):
    blocks, (pred_ref, dq_ref, dk_ref, dv_ref, view) = rest[:cams], rest[cams:]
    time = (t0, t1)
    share = blocks[0].shape[0]
    for d, part in enumerate(blocks):
        view[pl.ds(pl.multiple_of((cam[0] ^ d) * share, share), share), :] = part[...]
    rows = view.shape[0]
    frames = rows // 8
    row = iota((rows, rows), 0)
    col = iota((rows, rows), 1)
    source = (((row % 8) // 4) ^ (me[0] % 2)) * 4 * frames + (row // 8) * 4 + row % 4
    perm = jnp.where(col == source, 1.0, 0.0).astype(BF)
    for i, ref in enumerate((dq_ref, dk_ref, dv_ref), 1):
        part = slice(i * CW, (i + 1) * CW)
        ref[:, :CW] = view[:, part]
        ref[:, CW:] = dot_nn(perm, rows_of(time, part)).astype(BF)
    attn_time = dot_nn(perm, rows_of(time, slice(0, CW))).astype(BF)
    mixed = dot_nn(view[:, :CW], w[:CW]) + dot_nn(attn_time, w[CW:])
    total = mixed.reshape(frames, 8, 2 * CW) + action[...][:, None, :]
    pred_ref[...] = total.reshape(rows, 2 * CW).astype(BF)


def whole(shape):
    return pl.BlockSpec(shape, lambda *at: (0,) * len(shape))


def call(kernel, outs, specs, *args, scratch=(), kept=0):
    specs = [whole(arg.shape) if spec is VM else spec for spec, arg in zip(specs, args)]
    count = len(outs) - kept
    return list(
        pl.pallas_call(
            kernel,
            out_shape=[jax.ShapeDtypeStruct(shape, kind) for shape, kind in outs],
            in_specs=specs,
            out_specs=[whole(shape) for shape, _ in outs[:count]] + [ANY] * kept,
            grid=(1,),
            scratch_shapes=list(scratch),
            compiler_params=pltpu.CompilerParams(vmem_limit_bytes=56 * 1024 * 1024),
        )(*args)
    )


def shards(queries, keys, values, cam_valid, windows, actions, act_table, w_out, cotangent):
    _, frames, tokens, width = queries.shape
    rows = frames * tokens
    block = rows // PAIR
    cams = lax.axis_size("cam")
    tm = lax.axis_size("tm")
    at_tm = lax.axis_index("tm")
    core = at_tm % 2
    me = (at_tm % GROUP).reshape(1)
    pair = (at_tm // PAIR).reshape(1)
    group = (at_tm // GROUP).reshape(1)
    depth = tm // GROUP
    same_core = [[2 * i + j for i in range(tm // 2)] for j in range(2)]
    up = [(i, (i + GROUP) % tm) for i in range(tm)]
    down = [(i, (i - GROUP) % tm) for i in range(tm)]
    swap = [(i, i ^ 1) for i in range(tm)]
    beside = [(i, i ^ (tm + 2)) for i in range(cams * tm)]

    w_beside = lax.ppermute(w_out, ("cam", "tm"), beside)
    q, k, v, ct = (a.reshape(rows, width) for a in (queries, keys, values, cotangent))
    packed = call(
        pack_kernel,
        [((rows, 5 * CW + 128), BF)] + [((block, 2 * CW), BF)] * PAIR + [((block, 3 * CW), BF)] * PAIR,
        [SM, SM] + [ANY] * 4,
        me, cam_valid, q, k, v, ct,
        scratch=[pltpu.VMEM((4, rows, width), BF), pltpu.SemaphoreType.DMA((4,))],
    )
    view_send, kv, qct = packed[0], packed[1 : PAIR + 1], packed[PAIR + 1 :]
    w_beside, view_send = lax.optimization_barrier((w_beside, view_send))
    w_both = jnp.concatenate([w_out, w_beside], axis=0)
    view_x = lax.all_to_all(view_send, "cam", 0, 0, tiled=True)
    w_own, w_other = [w_both], []

    def pass_on(first, last):
        for i in range(first, min(last, depth)):
            w_own.append(lax.ppermute(w_own[max(i - 2, 0)], "tm", up if i % 2 else down))

    def swap_blocks(last):
        for block_rows in w_own[len(w_other) : last]:
            w_other.append(lax.ppermute(block_rows, "tm", swap))

    def tie(value):
        value, w_own[:], w_other[:] = lax.optimization_barrier((value, w_own[:], w_other[:]))
        return value

    own = jnp.concatenate([kv[0], lax.ppermute(kv[1], "tm", swap)], axis=0)
    q0, q1 = qct[0], lax.ppermute(qct[1], "tm", swap)

    own = tie(own)
    near = lax.ppermute(own, "tm", [(i, i + 2) for i in range(tm - 2)])
    far = lax.ppermute(own, "tm", [(i, i + 4) for i in range(tm - 4)])
    pass_on(1, 3)
    (action_sum,) = call(action_kernel, [((frames, width), F32)], [VM] * 2, actions, act_table)
    near, far = tie((near, far))
    pass_on(3, 5)
    swap_blocks(1)
    view_x = tie(view_x)
    pass_on(5, 7)
    swap_blocks(5)
    kept_view, view_swap, prob_view = call(
        view_forward_kernel,
        [((rows, 2 * CW), BF)] * 2 + [((PAIRS, 2 * rows, rows), F32)],
        [SM, VM],
        me, view_x,
    )
    kept_time, time_swap, prob_time = call(
        time_forward_kernel,
        [((rows, 2 * CW), BF)] * 2 + [((PAIRS, 2 * rows, 3 * rows), F32)],
        [SM] * 3 + [VM] * 5,
        windows, me, pair, q0, q1, far, near, own,
    )

    pass_on(7, depth)
    w_own[-1], action_sum = lax.optimization_barrier((w_own[-1], action_sum))
    swap_blocks(depth)
    view_swap = lax.ppermute(view_swap, "tm", swap)
    time_swap = lax.ppermute(time_swap, "tm", swap)
    grad_norm = 1.0 / math.sqrt(cams * tm * rows)
    (part,) = call(
        functools.partial(weight_kernel, grad_norm),
        [((width, CW), BF)],
        [VM] * 4,
        kept_view, view_swap, kept_time, time_swap,
    )
    part = lax.all_to_all(part.reshape(cams, width // cams, CW), "cam", 0, 0, tiled=True)

    dq_time, own_grad, near_grad, far_grad, w_full = call(
        functools.partial(time_backward_kernel, depth),
        [((rows, CW), BF), ((rows, 2 * CW), F32)] + [((rows, 2 * CW), BF)] * 2 + [((width, width), BF)],
        [SM] * 2 + [VM] * 6 + [ANY] * (2 * depth),
        me, group, q0, q1, far, near, own, prob_time, *w_own, *w_other,
        scratch=[pltpu.VMEM((width, width), BF), pltpu.SemaphoreType.DMA((tm,)), pltpu.SemaphoreType.DMA],
        kept=1,
    )
    part, near_grad = lax.optimization_barrier((part, near_grad))
    chips = tm // 2
    (part,) = call(
        camera_sum_kernel,
        [((chips, width // cams // chips, CW), BF)],
        [VM],
        part,
        scratch=[pltpu.VMEM((width // cams, CW), F32)],
    )
    view_x, part = lax.optimization_barrier((view_x, part))
    part = lax.all_to_all(part, "tm", 0, 0, tiled=True, axis_index_groups=same_core)
    near_grad = lax.ppermute(near_grad, "tm", [(i + 2, i) for i in range(tm - 2)])
    far_grad = lax.ppermute(far_grad, "tm", [(i + 4, i) for i in range(tm - 4)])
    cam = lax.axis_index("cam").reshape(1)
    view_out = call(
        view_backward_kernel,
        [((rows // cams, 4 * CW), BF)] * cams,
        [SM] + [VM] * 3 + [pl.BlockSpec((CW, width), lambda *at: (0, 0))],
        cam, view_x, kept_view, prob_view, w_full,
        scratch=[pltpu.VMEM((rows, 4 * CW), BF)],
    )
    view_back = [view_out[0]] + [
        lax.ppermute(view_out[d], "cam", [(i, i ^ d) for i in range(cams)]) for d in range(1, cams)
    ]

    part, near_grad, far_grad, view_back[1:4] = lax.optimization_barrier(
        (part, near_grad, far_grad, view_back[1:4])
    )
    part = jnp.sum(part.astype(F32), axis=0)
    final = width // cams // tm
    mine = lax.dynamic_slice_in_dim(part, core * final, final, 0)
    theirs = lax.ppermute(lax.dynamic_slice_in_dim(part, (1 - core) * final, final, 0), "tm", swap)
    grad_out_weight = jnp.concatenate(
        [jnp.where(core == 0, mine, theirs), jnp.where(core == 0, theirs, mine)], axis=1
    )

    t0, t1 = call(
        time_sum_kernel, [((block, 4 * CW), BF)] * PAIR, [VM] * 5, kept_time, dq_time, own_grad, near_grad, far_grad
    )
    t1 = lax.ppermute(t1, "tm", swap)
    outs = call(
        functools.partial(finish_kernel, cams),
        [((rows, width), BF)] * 4,
        [SM] * 2 + [VM] * (4 + cams),
        me, cam, w_full, action_sum, t0, t1, *view_back,
        scratch=[pltpu.VMEM((rows, 4 * CW), BF)],
    )
    return tuple(a.reshape(1, frames, tokens, width) for a in outs) + (grad_out_weight,)


def solution(mesh):
    in_specs = (
        P("cam", "tm", None, None),
        P("cam", "tm", None, None),
        P("cam", "tm", None, None),
        P("cam", "tm"),
        P(),
        P("tm", None),
        P(),
        P("tm", None),
        P("cam", "tm", None, None),
    )
    out_specs = (
        P("cam", "tm", None, None),
        P("cam", "tm", None, None),
        P("cam", "tm", None, None),
        P("cam", "tm", None, None),
        P(("cam", "tm"), None),
    )
    return jax.shard_map(shards, mesh=mesh, in_specs=in_specs, out_specs=out_specs, check_vma=False)
```

```python
import functools
import math

import jax
import jax.numpy as jnp
from jax import lax
from jax.experimental import pallas as pl
from jax.experimental.pallas import tpu as pltpu
from jax.sharding import PartitionSpec as P

HC = 12
HT = 12
HD = 64
WIN = 64
CW = HC * HD
GROUP = 4
PAIR = 2
SCALE = HD ** (-0.5)
BF = jnp.bfloat16
F32 = jnp.float32
PAIRS = HC // 2
VM = pl.BlockSpec(memory_space=pltpu.VMEM)
ANY = pl.BlockSpec(memory_space=pl.ANY)
SM = pl.BlockSpec(memory_space=pltpu.SMEM)


def iota(shape, dim):
    return lax.broadcasted_iota(jnp.int32, shape, dim)


def dot_nt(a, b):
    return lax.dot_general(a, b, (((1,), (1,)), ((), ())), preferred_element_type=F32)


def dot_tn(a, b):
    return lax.dot_general(a, b, (((0,), (0,)), ((), ())), preferred_element_type=F32)


def dot_nn(a, b):
    return jnp.dot(a, b, preferred_element_type=F32)


def split_pair(rows):
    low = iota(rows.shape, 1) < HD
    zero = jnp.zeros_like(rows)
    return jnp.concatenate([jnp.where(low, rows, zero), jnp.where(low, zero, rows)], axis=0)


def join_pair(rows):
    count = rows.shape[0] // 2
    low = iota((count, rows.shape[1]), 1) < HD
    return jnp.where(low, rows[:count], rows[count:])


def softmax_pair(q, k, mask):
    scores = dot_nt(split_pair(q), k) * SCALE
    scores = jnp.where(mask, scores, -jnp.inf)
    largest = jnp.max(scores, axis=1, keepdims=True)
    e = jnp.exp(scores - largest)
    return e / jnp.sum(e, axis=1, keepdims=True)


def pack_kernel(me, valid, q, k, v, ct, view_ref, *rest):
    kv_refs, qct_refs, (held, sems) = rest[:PAIR], rest[PAIR : 2 * PAIR], rest[2 * PAIR :]
    copies = [pltpu.make_async_copy(ref, held.at[i], sems.at[i]) for i, ref in enumerate((q, k, v, ct))]
    for copy in copies:
        copy.start()
    rows = q.shape[0]
    frames = rows // 8
    block = 4 * frames
    row = iota((rows, rows), 0)
    col = iota((rows, rows), 1)
    source = ((row // 4) % frames) * 8 + 4 * ((row // block) ^ (me[0] % 2)) + row % 4
    perm = jnp.where(col == source, 1.0, 0.0).astype(BF)
    frame = iota((rows, 128), 0) // 8
    flags = jnp.zeros((rows, 128), F32)
    for f in range(frames):
        flags = jnp.where(frame == f, valid[0, f].astype(F32), flags)
    view_ref[:, 5 * CW :] = jnp.where(flags > 0.5, 1.0, 0.0).astype(BF)
    for i in range(4):
        copies[i].wait()
        if i < 3:
            view_ref[:, i * CW : (i + 1) * CW] = held[i, :, :CW]
            moved = dot_nn(perm, held[i, :, CW:]).astype(BF)
        else:
            view_ref[:, 3 * CW : 5 * CW] = held[i]
            moved = dot_nn(perm, held[i]).astype(BF)
        for d in range(PAIR):
            part = moved[d * block : (d + 1) * block]
            if i in (1, 2):
                kv_refs[d][:, (i - 1) * CW : i * CW] = part
            elif i == 0:
                qct_refs[d][:, :CW] = part
            else:
                qct_refs[d][:, CW:] = part


def view_mask(flags):
    rows = flags.shape[0]
    pick = jnp.where(iota((8, 128), 1) == 0, 1.0, 0.0).astype(BF)
    valid_row = dot_nt(pick, flags)[:1]
    r = iota((2 * rows, rows), 0) % rows
    c = iota((2 * rows, rows), 1)
    same_frame = ((r // 8) % 2) == ((c // 8) % 2)
    return same_frame & ((valid_row > 0.5) | (r // 16 == c // 16))


def keep_for_weight(attn, ct, core, own_ref, send_ref):
    own_ref[:, :CW] = attn
    send_ref[:, :CW] = attn
    own_ref[:, CW:] = jnp.where(core == 0, ct[:, :CW], ct[:, CW:])
    send_ref[:, CW:] = jnp.where(core == 0, ct[:, CW:], ct[:, :CW])


def view_forward_kernel(me, x, own_ref, send_ref, prob_ref):
    mask = view_mask(x[:, 5 * CW :])
    attn = []
    for j in range(PAIRS):
        q = x[:, 128 * j : 128 * (j + 1)]
        k = x[:, CW + 128 * j : CW + 128 * (j + 1)]
        v = x[:, 2 * CW + 128 * j : 2 * CW + 128 * (j + 1)]
        prob = softmax_pair(q, k, mask)
        prob_ref[j] = prob
        attn.append(join_pair(dot_nn(prob.astype(BF), v)).astype(BF))
    keep_for_weight(jnp.concatenate(attn, axis=1), x[:, 3 * CW : 5 * CW], me[0] % 2, own_ref, send_ref)


def rows_of(refs, columns):
    return jnp.concatenate([ref[:, columns] for ref in refs], axis=0)


def time_forward_kernel(windows, me, pair, q0, q1, far, near, own, own_ref, send_ref, prob_ref):
    qct, kv = (q0, q1), (far, near, own)
    size = q0.shape[0]
    rows = PAIR * size
    shape = (2 * rows, 3 * rows)
    r = iota(shape, 0)
    c = iota(shape, 1)
    second = r >= rows
    core = me[0] % 2
    span = size // 2

    def frame_of(row):
        return ((row // size) ^ core) * (size // 4) + (row % size) // 4

    key_frame = frame_of(c % rows) + span * (c // rows) - 2 * span
    gap = frame_of(r % rows) - key_frame
    base = (r % 4 == c % 4) & (gap >= 0) & (key_frame + span * pair[0] >= 0)
    attn = []
    for j in range(PAIRS):
        at = [slice(i * CW + 128 * j, i * CW + 128 * (j + 1)) for i in range(2)]
        limit = jnp.where(second, windows[2 * j + 1], windows[2 * j])
        prob = softmax_pair(rows_of(qct, at[0]), rows_of(kv, at[0]), base & (gap < limit))
        prob_ref[j] = prob
        attn.append(join_pair(dot_nn(prob.astype(BF), rows_of(kv, at[1]))).astype(BF))
    keep_for_weight(jnp.concatenate(attn, axis=1), rows_of(qct, slice(CW, 3 * CW)), core, own_ref, send_ref)


def weight_kernel(scale, own_view, other_view, own_time, other_time, out_ref):
    for i, (own, other) in enumerate(((own_view, other_view), (own_time, other_time))):
        left = jnp.concatenate([own[:, :CW], other[:, :CW]], axis=0)
        right = jnp.concatenate([own[:, CW:], other[:, CW:]], axis=0)
        out_ref[i * CW : (i + 1) * CW, :] = (dot_tn(left, right) * scale).astype(BF)


def fetch_weight(me, z, own, others, held, sem):
    depth = len(own)
    size = own[0].shape[0] // 2
    core, y = me[0] % 2, me[0] // 2
    copies = []
    for i in range(depth):
        place = lax.rem(z[0] + offset(i, depth), depth)
        for n, (which, ref) in enumerate(((core, own[i]), (1 - core, others[i]))):
            for e in range(2):
                start = pl.multiple_of((4 * place + 2 * (y ^ e) + which) * size, 16)
                copies.append(
                    pltpu.make_async_copy(
                        ref.at[pl.ds(e * size, size)], held.at[pl.ds(start, size)], sem.at[4 * i + 2 * n + e]
                    )
                )
    for copy in copies:
        copy.start()
    return copies


def offset(i, depth):
    return (i + 1) // 2 if i % 2 == 0 else depth - (i + 1) // 2


def backward_pair(q, k, v, g, prob):
    g2 = split_pair(g)
    grad_prob = dot_nt(g2, v)
    total = jnp.sum(prob * grad_prob, axis=1, keepdims=True)
    grad_scores = (prob * (grad_prob - total)).astype(BF)
    dq = join_pair(dot_nn(grad_scores, k)) * SCALE
    dk = dot_tn(grad_scores, split_pair(q)) * SCALE
    dv = dot_tn(prob.astype(BF), g2)
    return dq, dk, dv


def time_backward_kernel(depth, me, z, q0, q1, far, near, own, prob_ref, *rest):
    w_own, w_other, rest = rest[:depth], rest[depth : 2 * depth], rest[2 * depth :]
    dq_ref, own_ref, near_ref, far_ref, full_ref, w, sem, full_sem = rest
    copies = fetch_weight(me, z, w_own, w_other, w, sem)
    qct, kv = (q0, q1), (far, near, own)
    rows = PAIR * q0.shape[0]
    for copy in copies:
        copy.wait()
    full = pltpu.make_async_copy(w, full_ref, full_sem)
    full.start()
    grad = dot_nt(rows_of(qct, slice(CW, 3 * CW)), w[CW:]).astype(BF)
    for j in range(PAIRS):
        at = [slice(i * CW + 128 * j, i * CW + 128 * (j + 1)) for i in range(2)]
        dq, dk, dv = backward_pair(
            rows_of(qct, at[0]), rows_of(kv, at[0]), rows_of(kv, at[1]), grad[:, at[0]], prob_ref[j]
        )
        dq_ref[:, at[0]] = dq.astype(BF)
        for part, value in zip(at, (dk, dv)):
            far_ref[:, part] = value[:rows].astype(BF)
            near_ref[:, part] = value[rows : 2 * rows].astype(BF)
            own_ref[:, part] = value[2 * rows :]
    full.wait()


def view_backward_kernel(cam, x, kept, prob_ref, w, *rest):
    out_refs, held = rest[:-1], rest[-1]
    held[:, :CW] = kept[:, :CW]
    grad = dot_nt(x[:, 3 * CW : 5 * CW], w[...]).astype(BF)
    for j in range(PAIRS):
        at = [slice(i * CW + 128 * j, i * CW + 128 * (j + 1)) for i in range(4)]
        dq, dk, dv = backward_pair(x[:, at[0]], x[:, at[1]], x[:, at[2]], grad[:, at[0]], prob_ref[j])
        held[:, at[1]] = dq.astype(BF)
        held[:, at[2]] = dk.astype(BF)
        held[:, at[3]] = dv.astype(BF)
    size = held.shape[0] // len(out_refs)
    for d, out in enumerate(out_refs):
        out[...] = held[pl.ds(pl.multiple_of((cam[0] ^ d) * size, size), size), :]


def time_sum_kernel(kept, dq, own, near, far, *outs):
    size = outs[0].shape[0]
    for d, out in enumerate(outs):
        part = slice(d * size, (d + 1) * size)
        out[:, :CW] = kept[part, :CW]
        out[:, CW : 2 * CW] = dq[part]
        out[:, 2 * CW :] = (own[part] + near[part].astype(F32) + far[part].astype(F32)).astype(BF)


def action_kernel(actions, table, out_ref):
    total = None
    for d in range(table.shape[0]):
        codes = iota((actions.shape[0], table.shape[1]), 1)
        one_hot = jnp.where(actions[:, d : d + 1] == codes, 1.0, 0.0).astype(BF)
        term = dot_nn(one_hot, table[d])
        total = term if total is None else total + term
    out_ref[...] = total


def camera_sum_kernel(parts, out_ref, held):
    total = parts[0].astype(F32)
    for i in range(1, parts.shape[0]):
        total = total + parts[i].astype(F32)
    held[...] = total
    size = out_ref.shape[1]
    for i in range(out_ref.shape[0]):
        out_ref[i] = held[i * size : (i + 1) * size, :].astype(BF)


def finish_kernel(cams, me, cam, w, action, t0, t1, *rest):
    blocks, (pred_ref, dq_ref, dk_ref, dv_ref, view) = rest[:cams], rest[cams:]
    time = (t0, t1)
    share = blocks[0].shape[0]
    for d, part in enumerate(blocks):
        view[pl.ds(pl.multiple_of((cam[0] ^ d) * share, share), share), :] = part[...]
    rows = view.shape[0]
    frames = rows // 8
    row = iota((rows, rows), 0)
    col = iota((rows, rows), 1)
    source = (((row % 8) // 4) ^ (me[0] % 2)) * 4 * frames + (row // 8) * 4 + row % 4
    perm = jnp.where(col == source, 1.0, 0.0).astype(BF)
    for i, ref in enumerate((dq_ref, dk_ref, dv_ref), 1):
        part = slice(i * CW, (i + 1) * CW)
        ref[:, :CW] = view[:, part]
        ref[:, CW:] = dot_nn(perm, rows_of(time, part)).astype(BF)
    attn_time = dot_nn(perm, rows_of(time, slice(0, CW))).astype(BF)
    mixed = dot_nn(view[:, :CW], w[:CW]) + dot_nn(attn_time, w[CW:])
    total = mixed.reshape(frames, 8, 2 * CW) + action[...][:, None, :]
    pred_ref[...] = total.reshape(rows, 2 * CW).astype(BF)


def whole(shape):
    return pl.BlockSpec(shape, lambda *at: (0,) * len(shape))


def call(kernel, outs, specs, *args, scratch=(), kept=0):
    specs = [whole(arg.shape) if spec is VM else spec for spec, arg in zip(specs, args)]
    count = len(outs) - kept
    return list(
        pl.pallas_call(
            kernel,
            out_shape=[jax.ShapeDtypeStruct(shape, kind) for shape, kind in outs],
            in_specs=specs,
            out_specs=[whole(shape) for shape, _ in outs[:count]] + [ANY] * kept,
            grid=(1,),
            scratch_shapes=list(scratch),
            compiler_params=pltpu.CompilerParams(vmem_limit_bytes=56 * 1024 * 1024),
        )(*args)
    )


def shards(queries, keys, values, cam_valid, windows, actions, act_table, w_out, cotangent):
    _, frames, tokens, width = queries.shape
    rows = frames * tokens
    block = rows // PAIR
    cams = lax.axis_size("cam")
    tm = lax.axis_size("tm")
    at_tm = lax.axis_index("tm")
    core = at_tm % 2
    me = (at_tm % GROUP).reshape(1)
    pair = (at_tm // PAIR).reshape(1)
    group = (at_tm // GROUP).reshape(1)
    depth = tm // GROUP
    same_core = [[2 * i + j for i in range(tm // 2)] for j in range(2)]
    up = [(i, (i + GROUP) % tm) for i in range(tm)]
    down = [(i, (i - GROUP) % tm) for i in range(tm)]
    swap = [(i, i ^ 1) for i in range(tm)]
    beside = [(i, i ^ (tm + 2)) for i in range(cams * tm)]

    w_beside = lax.ppermute(w_out, ("cam", "tm"), beside)
    q, k, v, ct = (a.reshape(rows, width) for a in (queries, keys, values, cotangent))
    packed = call(
        pack_kernel,
        [((rows, 5 * CW + 128), BF)] + [((block, 2 * CW), BF)] * PAIR + [((block, 3 * CW), BF)] * PAIR,
        [SM, SM] + [ANY] * 4,
        me, cam_valid, q, k, v, ct,
        scratch=[pltpu.VMEM((4, rows, width), BF), pltpu.SemaphoreType.DMA((4,))],
    )
    view_send, kv, qct = packed[0], packed[1 : PAIR + 1], packed[PAIR + 1 :]
    w_beside, view_send = lax.optimization_barrier((w_beside, view_send))
    w_both = jnp.concatenate([w_out, w_beside], axis=0)
    view_x = lax.all_to_all(view_send, "cam", 0, 0, tiled=True)
    w_own, w_other = [w_both], []

    def pass_on(first, last):
        for i in range(first, min(last, depth)):
            w_own.append(lax.ppermute(w_own[max(i - 2, 0)], "tm", up if i % 2 else down))

    def swap_blocks(last):
        for block_rows in w_own[len(w_other) : last]:
            w_other.append(lax.ppermute(block_rows, "tm", swap))

    def tie(value):
        value, w_own[:], w_other[:] = lax.optimization_barrier((value, w_own[:], w_other[:]))
        return value

    own = jnp.concatenate([kv[0], lax.ppermute(kv[1], "tm", swap)], axis=0)
    q0, q1 = qct[0], lax.ppermute(qct[1], "tm", swap)

    own = tie(own)
    near = lax.ppermute(own, "tm", [(i, i + 2) for i in range(tm - 2)])
    far = lax.ppermute(own, "tm", [(i, i + 4) for i in range(tm - 4)])
    pass_on(1, 3)
    (action_sum,) = call(action_kernel, [((frames, width), F32)], [VM] * 2, actions, act_table)
    near, far = tie((near, far))
    pass_on(3, 5)
    swap_blocks(1)
    view_x = tie(view_x)
    pass_on(5, 7)
    swap_blocks(5)
    kept_view, view_swap, prob_view = call(
        view_forward_kernel,
        [((rows, 2 * CW), BF)] * 2 + [((PAIRS, 2 * rows, rows), F32)],
        [SM, VM],
        me, view_x,
    )
    kept_time, time_swap, prob_time = call(
        time_forward_kernel,
        [((rows, 2 * CW), BF)] * 2 + [((PAIRS, 2 * rows, 3 * rows), F32)],
        [SM] * 3 + [VM] * 5,
        windows, me, pair, q0, q1, far, near, own,
    )

    pass_on(7, depth)
    w_own[-1], action_sum = lax.optimization_barrier((w_own[-1], action_sum))
    swap_blocks(depth)
    view_swap = lax.ppermute(view_swap, "tm", swap)
    time_swap = lax.ppermute(time_swap, "tm", swap)
    grad_norm = 1.0 / math.sqrt(cams * tm * rows)
    (part,) = call(
        functools.partial(weight_kernel, grad_norm),
        [((width, CW), BF)],
        [VM] * 4,
        kept_view, view_swap, kept_time, time_swap,
    )
    part = lax.all_to_all(part.reshape(cams, width // cams, CW), "cam", 0, 0, tiled=True)

    dq_time, own_grad, near_grad, far_grad, w_full = call(
        functools.partial(time_backward_kernel, depth),
        [((rows, CW), BF), ((rows, 2 * CW), F32)] + [((rows, 2 * CW), BF)] * 2 + [((width, width), BF)],
        [SM] * 2 + [VM] * 6 + [ANY] * (2 * depth),
        me, group, q0, q1, far, near, own, prob_time, *w_own, *w_other,
        scratch=[pltpu.VMEM((width, width), BF), pltpu.SemaphoreType.DMA((tm,)), pltpu.SemaphoreType.DMA],
        kept=1,
    )
    view_x, near_grad = lax.optimization_barrier((view_x, near_grad))
    near_grad = lax.ppermute(near_grad, "tm", [(i + 2, i) for i in range(tm - 2)])
    far_grad = lax.ppermute(far_grad, "tm", [(i + 4, i) for i in range(tm - 4)])
    cam = lax.axis_index("cam").reshape(1)
    view_out = call(
        view_backward_kernel,
        [((rows // cams, 4 * CW), BF)] * cams,
        [SM] + [VM] * 3 + [pl.BlockSpec((CW, width), lambda *at: (0, 0))],
        cam, view_x, kept_view, prob_view, w_full,
        scratch=[pltpu.VMEM((rows, 4 * CW), BF)],
    )
    part, view_out[0] = lax.optimization_barrier((part, view_out[0]))
    chips = tm // 2
    (part,) = call(
        camera_sum_kernel,
        [((chips, width // cams // chips, CW), BF)],
        [VM],
        part,
        scratch=[pltpu.VMEM((width // cams, CW), F32)],
    )
    part = lax.all_to_all(part, "tm", 0, 0, tiled=True, axis_index_groups=same_core)
    view_back = [view_out[0]] + [
        lax.ppermute(view_out[d], "cam", [(i, i ^ d) for i in range(cams)]) for d in range(1, cams)
    ]

    part, near_grad, far_grad, view_back[1:4] = lax.optimization_barrier(
        (part, near_grad, far_grad, view_back[1:4])
    )
    part = jnp.sum(part.astype(F32), axis=0)
    final = width // cams // tm
    mine = lax.dynamic_slice_in_dim(part, core * final, final, 0)
    theirs = lax.ppermute(lax.dynamic_slice_in_dim(part, (1 - core) * final, final, 0), "tm", swap)
    grad_out_weight = jnp.concatenate(
        [jnp.where(core == 0, mine, theirs), jnp.where(core == 0, theirs, mine)], axis=1
    )

    t0, t1 = call(
        time_sum_kernel, [((block, 4 * CW), BF)] * PAIR, [VM] * 5, kept_time, dq_time, own_grad, near_grad, far_grad
    )
    t1 = lax.ppermute(t1, "tm", swap)
    outs = call(
        functools.partial(finish_kernel, cams),
        [((rows, width), BF)] * 4,
        [SM] * 2 + [VM] * (4 + cams),
        me, cam, w_full, action_sum, t0, t1, *view_back,
        scratch=[pltpu.VMEM((rows, 4 * CW), BF)],
    )
    return tuple(a.reshape(1, frames, tokens, width) for a in outs) + (grad_out_weight,)


def solution(mesh):
    in_specs = (
        P("cam", "tm", None, None),
        P("cam", "tm", None, None),
        P("cam", "tm", None, None),
        P("cam", "tm"),
        P(),
        P("tm", None),
        P(),
        P("tm", None),
        P("cam", "tm", None, None),
    )
    out_specs = (
        P("cam", "tm", None, None),
        P("cam", "tm", None, None),
        P("cam", "tm", None, None),
        P("cam", "tm", None, None),
        P(("cam", "tm"), None),
    )
    return jax.shard_map(shards, mesh=mesh, in_specs=in_specs, out_specs=out_specs, check_vma=False)
```

```python
import functools
import math

import jax
import jax.numpy as jnp
from jax import lax
from jax.experimental import pallas as pl
from jax.experimental.pallas import tpu as pltpu
from jax.sharding import PartitionSpec as P

HC = 12
HT = 12
HD = 64
WIN = 64
CW = HC * HD
GROUP = 4
PAIR = 2
SCALE = HD ** (-0.5)
BF = jnp.bfloat16
F32 = jnp.float32
PAIRS = HC // 2
VM = pl.BlockSpec(memory_space=pltpu.VMEM)
ANY = pl.BlockSpec(memory_space=pl.ANY)
SM = pl.BlockSpec(memory_space=pltpu.SMEM)


def iota(shape, dim):
    return lax.broadcasted_iota(jnp.int32, shape, dim)


def dot_nt(a, b):
    return lax.dot_general(a, b, (((1,), (1,)), ((), ())), preferred_element_type=F32)


def dot_tn(a, b):
    return lax.dot_general(a, b, (((0,), (0,)), ((), ())), preferred_element_type=F32)


def dot_nn(a, b):
    return jnp.dot(a, b, preferred_element_type=F32)


def split_pair(rows):
    low = iota(rows.shape, 1) < HD
    zero = jnp.zeros_like(rows)
    return jnp.concatenate([jnp.where(low, rows, zero), jnp.where(low, zero, rows)], axis=0)


def join_pair(rows):
    count = rows.shape[0] // 2
    low = iota((count, rows.shape[1]), 1) < HD
    return jnp.where(low, rows[:count], rows[count:])


def softmax_pair(q, k, mask):
    scores = dot_nt(split_pair(q), k) * SCALE
    scores = jnp.where(mask, scores, -jnp.inf)
    largest = jnp.max(scores, axis=1, keepdims=True)
    e = jnp.exp(scores - largest)
    return e / jnp.sum(e, axis=1, keepdims=True)


def pack_kernel(me, valid, q, k, v, ct, view_ref, *rest):
    kv_refs, qct_refs, (held, sems) = rest[:PAIR], rest[PAIR : 2 * PAIR], rest[2 * PAIR :]
    copies = [pltpu.make_async_copy(ref, held.at[i], sems.at[i]) for i, ref in enumerate((q, k, v, ct))]
    for copy in copies:
        copy.start()
    rows = q.shape[0]
    frames = rows // 8
    block = 4 * frames
    row = iota((rows, rows), 0)
    col = iota((rows, rows), 1)
    source = ((row // 4) % frames) * 8 + 4 * ((row // block) ^ (me[0] % 2)) + row % 4
    perm = jnp.where(col == source, 1.0, 0.0).astype(BF)
    frame = iota((rows, 128), 0) // 8
    flags = jnp.zeros((rows, 128), F32)
    for f in range(frames):
        flags = jnp.where(frame == f, valid[0, f].astype(F32), flags)
    view_ref[:, 5 * CW :] = jnp.where(flags > 0.5, 1.0, 0.0).astype(BF)
    for i in range(4):
        copies[i].wait()
        if i < 3:
            view_ref[:, i * CW : (i + 1) * CW] = held[i, :, :CW]
            moved = dot_nn(perm, held[i, :, CW:]).astype(BF)
        else:
            view_ref[:, 3 * CW : 5 * CW] = held[i]
            moved = dot_nn(perm, held[i]).astype(BF)
        for d in range(PAIR):
            part = moved[d * block : (d + 1) * block]
            if i in (1, 2):
                kv_refs[d][:, (i - 1) * CW : i * CW] = part
            elif i == 0:
                qct_refs[d][:, :CW] = part
            else:
                qct_refs[d][:, CW:] = part


def view_mask(flags):
    rows = flags.shape[0]
    pick = jnp.where(iota((8, 128), 1) == 0, 1.0, 0.0).astype(BF)
    valid_row = dot_nt(pick, flags)[:1]
    r = iota((2 * rows, rows), 0) % rows
    c = iota((2 * rows, rows), 1)
    same_frame = ((r // 8) % 2) == ((c // 8) % 2)
    return same_frame & ((valid_row > 0.5) | (r // 16 == c // 16))


def keep_for_weight(attn, ct, core, own_ref, send_ref):
    own_ref[:, :CW] = attn
    send_ref[:, :CW] = attn
    own_ref[:, CW:] = jnp.where(core == 0, ct[:, :CW], ct[:, CW:])
    send_ref[:, CW:] = jnp.where(core == 0, ct[:, CW:], ct[:, :CW])


def view_forward_kernel(me, x, own_ref, send_ref, prob_ref):
    mask = view_mask(x[:, 5 * CW :])
    attn = []
    for j in range(PAIRS):
        q = x[:, 128 * j : 128 * (j + 1)]
        k = x[:, CW + 128 * j : CW + 128 * (j + 1)]
        v = x[:, 2 * CW + 128 * j : 2 * CW + 128 * (j + 1)]
        prob = softmax_pair(q, k, mask)
        prob_ref[j] = prob
        attn.append(join_pair(dot_nn(prob.astype(BF), v)).astype(BF))
    keep_for_weight(jnp.concatenate(attn, axis=1), x[:, 3 * CW : 5 * CW], me[0] % 2, own_ref, send_ref)


def rows_of(refs, columns):
    return jnp.concatenate([ref[:, columns] for ref in refs], axis=0)


def time_forward_kernel(windows, me, pair, q0, q1, far, near, own, own_ref, send_ref, prob_ref):
    qct, kv = (q0, q1), (far, near, own)
    size = q0.shape[0]
    rows = PAIR * size
    shape = (2 * rows, 3 * rows)
    r = iota(shape, 0)
    c = iota(shape, 1)
    second = r >= rows
    core = me[0] % 2
    span = size // 2

    def frame_of(row):
        return ((row // size) ^ core) * (size // 4) + (row % size) // 4

    key_frame = frame_of(c % rows) + span * (c // rows) - 2 * span
    gap = frame_of(r % rows) - key_frame
    base = (r % 4 == c % 4) & (gap >= 0) & (key_frame + span * pair[0] >= 0)
    attn = []
    for j in range(PAIRS):
        at = [slice(i * CW + 128 * j, i * CW + 128 * (j + 1)) for i in range(2)]
        limit = jnp.where(second, windows[2 * j + 1], windows[2 * j])
        prob = softmax_pair(rows_of(qct, at[0]), rows_of(kv, at[0]), base & (gap < limit))
        prob_ref[j] = prob
        attn.append(join_pair(dot_nn(prob.astype(BF), rows_of(kv, at[1]))).astype(BF))
    keep_for_weight(jnp.concatenate(attn, axis=1), rows_of(qct, slice(CW, 3 * CW)), core, own_ref, send_ref)


def weight_kernel(scale, own_view, other_view, own_time, other_time, out_ref):
    for i, (own, other) in enumerate(((own_view, other_view), (own_time, other_time))):
        left = jnp.concatenate([own[:, :CW], other[:, :CW]], axis=0)
        right = jnp.concatenate([own[:, CW:], other[:, CW:]], axis=0)
        out_ref[i * CW : (i + 1) * CW, :] = (dot_tn(left, right) * scale).astype(BF)


def fetch_weight(me, z, own, others, held, sem):
    depth = len(own)
    size = own[0].shape[0] // 2
    core, y = me[0] % 2, me[0] // 2
    copies = []
    for i in range(depth):
        place = lax.rem(z[0] + offset(i, depth), depth)
        for n, (which, ref) in enumerate(((core, own[i]), (1 - core, others[i]))):
            for e in range(2):
                start = pl.multiple_of((4 * place + 2 * (y ^ e) + which) * size, 16)
                copies.append(
                    pltpu.make_async_copy(
                        ref.at[pl.ds(e * size, size)], held.at[pl.ds(start, size)], sem.at[4 * i + 2 * n + e]
                    )
                )
    for copy in copies:
        copy.start()
    return copies


def offset(i, depth):
    return (i + 1) // 2 if i % 2 == 0 else depth - (i + 1) // 2


def backward_pair(q, k, v, g, prob):
    g2 = split_pair(g)
    grad_prob = dot_nt(g2, v)
    total = jnp.sum(prob * grad_prob, axis=1, keepdims=True)
    grad_scores = (prob * (grad_prob - total)).astype(BF)
    dq = join_pair(dot_nn(grad_scores, k)) * SCALE
    dk = dot_tn(grad_scores, split_pair(q)) * SCALE
    dv = dot_tn(prob.astype(BF), g2)
    return dq, dk, dv


def time_backward_kernel(depth, me, z, q0, q1, far, near, own, prob_ref, *rest):
    w_own, w_other, rest = rest[:depth], rest[depth : 2 * depth], rest[2 * depth :]
    dq_ref, own_ref, near_ref, far_ref, full_ref, w, sem, full_sem = rest
    copies = fetch_weight(me, z, w_own, w_other, w, sem)
    qct, kv = (q0, q1), (far, near, own)
    rows = PAIR * q0.shape[0]
    for copy in copies:
        copy.wait()
    full = pltpu.make_async_copy(w, full_ref, full_sem)
    full.start()
    grad = dot_nt(rows_of(qct, slice(CW, 3 * CW)), w[CW:]).astype(BF)
    for j in range(PAIRS):
        at = [slice(i * CW + 128 * j, i * CW + 128 * (j + 1)) for i in range(2)]
        dq, dk, dv = backward_pair(
            rows_of(qct, at[0]), rows_of(kv, at[0]), rows_of(kv, at[1]), grad[:, at[0]], prob_ref[j]
        )
        dq_ref[:, at[0]] = dq.astype(BF)
        for part, value in zip(at, (dk, dv)):
            far_ref[:, part] = value[:rows].astype(BF)
            near_ref[:, part] = value[rows : 2 * rows].astype(BF)
            own_ref[:, part] = value[2 * rows :]
    full.wait()


def view_backward_kernel(cam, x, kept, prob_ref, w, *rest):
    out_refs, held = rest[:-1], rest[-1]
    held[:, :CW] = kept[:, :CW]
    grad = dot_nt(x[:, 3 * CW : 5 * CW], w[...]).astype(BF)
    for j in range(PAIRS):
        at = [slice(i * CW + 128 * j, i * CW + 128 * (j + 1)) for i in range(4)]
        dq, dk, dv = backward_pair(x[:, at[0]], x[:, at[1]], x[:, at[2]], grad[:, at[0]], prob_ref[j])
        held[:, at[1]] = dq.astype(BF)
        held[:, at[2]] = dk.astype(BF)
        held[:, at[3]] = dv.astype(BF)
    size = held.shape[0] // len(out_refs)
    for d, out in enumerate(out_refs):
        out[...] = held[pl.ds(pl.multiple_of((cam[0] ^ d) * size, size), size), :]


def time_sum_kernel(kept, dq, own, near, far, *outs):
    size = outs[0].shape[0]
    for d, out in enumerate(outs):
        part = slice(d * size, (d + 1) * size)
        out[:, :CW] = kept[part, :CW]
        out[:, CW : 2 * CW] = dq[part]
        out[:, 2 * CW :] = (own[part] + near[part].astype(F32) + far[part].astype(F32)).astype(BF)


def action_kernel(actions, table, out_ref):
    total = None
    for d in range(table.shape[0]):
        codes = iota((actions.shape[0], table.shape[1]), 1)
        one_hot = jnp.where(actions[:, d : d + 1] == codes, 1.0, 0.0).astype(BF)
        term = dot_nn(one_hot, table[d])
        total = term if total is None else total + term
    out_ref[...] = total


def camera_sum_kernel(parts, out_ref, held):
    total = parts[0].astype(F32)
    for i in range(1, parts.shape[0]):
        total = total + parts[i].astype(F32)
    held[...] = total
    size = out_ref.shape[1]
    for i in range(out_ref.shape[0]):
        out_ref[i] = held[i * size : (i + 1) * size, :].astype(BF)


def finish_kernel(cams, me, cam, w, action, t0, t1, *rest):
    blocks, (pred_ref, dq_ref, dk_ref, dv_ref, view) = rest[:cams], rest[cams:]
    time = (t0, t1)
    share = blocks[0].shape[0]
    for d, part in enumerate(blocks):
        view[pl.ds(pl.multiple_of((cam[0] ^ d) * share, share), share), :] = part[...]
    rows = view.shape[0]
    frames = rows // 8
    row = iota((rows, rows), 0)
    col = iota((rows, rows), 1)
    source = (((row % 8) // 4) ^ (me[0] % 2)) * 4 * frames + (row // 8) * 4 + row % 4
    perm = jnp.where(col == source, 1.0, 0.0).astype(BF)
    for i, ref in enumerate((dq_ref, dk_ref, dv_ref), 1):
        part = slice(i * CW, (i + 1) * CW)
        ref[:, :CW] = view[:, part]
        ref[:, CW:] = dot_nn(perm, rows_of(time, part)).astype(BF)
    attn_time = dot_nn(perm, rows_of(time, slice(0, CW))).astype(BF)
    mixed = dot_nn(view[:, :CW], w[:CW]) + dot_nn(attn_time, w[CW:])
    total = mixed.reshape(frames, 8, 2 * CW) + action[...][:, None, :]
    pred_ref[...] = total.reshape(rows, 2 * CW).astype(BF)


def whole(shape):
    return pl.BlockSpec(shape, lambda *at: (0,) * len(shape))


def call(kernel, outs, specs, *args, scratch=(), kept=0):
    specs = [whole(arg.shape) if spec is VM else spec for spec, arg in zip(specs, args)]
    count = len(outs) - kept
    return list(
        pl.pallas_call(
            kernel,
            out_shape=[jax.ShapeDtypeStruct(shape, kind) for shape, kind in outs],
            in_specs=specs,
            out_specs=[whole(shape) for shape, _ in outs[:count]] + [ANY] * kept,
            grid=(1,),
            scratch_shapes=list(scratch),
            compiler_params=pltpu.CompilerParams(vmem_limit_bytes=56 * 1024 * 1024),
        )(*args)
    )


def shards(queries, keys, values, cam_valid, windows, actions, act_table, w_out, cotangent):
    _, frames, tokens, width = queries.shape
    rows = frames * tokens
    block = rows // PAIR
    cams = lax.axis_size("cam")
    tm = lax.axis_size("tm")
    at_tm = lax.axis_index("tm")
    core = at_tm % 2
    me = (at_tm % GROUP).reshape(1)
    pair = (at_tm // PAIR).reshape(1)
    group = (at_tm // GROUP).reshape(1)
    depth = tm // GROUP
    same_core = [[2 * i + j for i in range(tm // 2)] for j in range(2)]
    up = [(i, (i + GROUP) % tm) for i in range(tm)]
    down = [(i, (i - GROUP) % tm) for i in range(tm)]
    swap = [(i, i ^ 1) for i in range(tm)]
    beside = [(i, i ^ (tm + 2)) for i in range(cams * tm)]

    w_beside = lax.ppermute(w_out, ("cam", "tm"), beside)
    q, k, v, ct = (a.reshape(rows, width) for a in (queries, keys, values, cotangent))
    packed = call(
        pack_kernel,
        [((rows, 5 * CW + 128), BF)] + [((block, 2 * CW), BF)] * PAIR + [((block, 3 * CW), BF)] * PAIR,
        [SM, SM] + [ANY] * 4,
        me, cam_valid, q, k, v, ct,
        scratch=[pltpu.VMEM((4, rows, width), BF), pltpu.SemaphoreType.DMA((4,))],
    )
    view_send, kv, qct = packed[0], packed[1 : PAIR + 1], packed[PAIR + 1 :]
    w_beside, view_send = lax.optimization_barrier((w_beside, view_send))
    w_both = jnp.concatenate([w_out, w_beside], axis=0)
    view_x = lax.all_to_all(view_send, "cam", 0, 0, tiled=True)
    w_own, w_other = [w_both], []

    def pass_on(first, last):
        for i in range(first, min(last, depth)):
            w_own.append(lax.ppermute(w_own[max(i - 2, 0)], "tm", up if i % 2 else down))

    def swap_blocks(last):
        for block_rows in w_own[len(w_other) : last]:
            w_other.append(lax.ppermute(block_rows, "tm", swap))

    def tie(value):
        value, w_own[:], w_other[:] = lax.optimization_barrier((value, w_own[:], w_other[:]))
        return value

    own = jnp.concatenate([kv[0], lax.ppermute(kv[1], "tm", swap)], axis=0)
    q0, q1 = qct[0], lax.ppermute(qct[1], "tm", swap)

    own = tie(own)
    near = lax.ppermute(own, "tm", [(i, i + 2) for i in range(tm - 2)])
    far = lax.ppermute(own, "tm", [(i, i + 4) for i in range(tm - 4)])
    pass_on(1, 3)
    (action_sum,) = call(action_kernel, [((frames, width), F32)], [VM] * 2, actions, act_table)
    near, far = tie((near, far))
    pass_on(3, 5)
    swap_blocks(1)
    view_x = tie(view_x)
    pass_on(5, 7)
    swap_blocks(5)
    kept_view, view_swap, prob_view = call(
        view_forward_kernel,
        [((rows, 2 * CW), BF)] * 2 + [((PAIRS, 2 * rows, rows), F32)],
        [SM, VM],
        me, view_x,
    )
    kept_time, time_swap, prob_time = call(
        time_forward_kernel,
        [((rows, 2 * CW), BF)] * 2 + [((PAIRS, 2 * rows, 3 * rows), F32)],
        [SM] * 3 + [VM] * 5,
        windows, me, pair, q0, q1, far, near, own,
    )

    kept_view, w_own[5:7] = lax.optimization_barrier((kept_view, w_own[5:7]))
    pass_on(7, depth)
    w_own[-1], action_sum = lax.optimization_barrier((w_own[-1], action_sum))
    swap_blocks(depth)
    view_swap = lax.ppermute(view_swap, "tm", swap)
    time_swap = lax.ppermute(time_swap, "tm", swap)
    grad_norm = 1.0 / math.sqrt(cams * tm * rows)
    (part,) = call(
        functools.partial(weight_kernel, grad_norm),
        [((width, CW), BF)],
        [VM] * 4,
        kept_view, view_swap, kept_time, time_swap,
    )
    part = lax.all_to_all(part.reshape(cams, width // cams, CW), "cam", 0, 0, tiled=True)

    dq_time, own_grad, near_grad, far_grad, w_full = call(
        functools.partial(time_backward_kernel, depth),
        [((rows, CW), BF), ((rows, 2 * CW), F32)] + [((rows, 2 * CW), BF)] * 2 + [((width, width), BF)],
        [SM] * 2 + [VM] * 6 + [ANY] * (2 * depth),
        me, group, q0, q1, far, near, own, prob_time, *w_own, *w_other,
        scratch=[pltpu.VMEM((width, width), BF), pltpu.SemaphoreType.DMA((tm,)), pltpu.SemaphoreType.DMA],
        kept=1,
    )
    view_x, near_grad = lax.optimization_barrier((view_x, near_grad))
    near_grad = lax.ppermute(near_grad, "tm", [(i + 2, i) for i in range(tm - 2)])
    far_grad = lax.ppermute(far_grad, "tm", [(i + 4, i) for i in range(tm - 4)])
    cam = lax.axis_index("cam").reshape(1)
    view_out = call(
        view_backward_kernel,
        [((rows // cams, 4 * CW), BF)] * cams,
        [SM] + [VM] * 3 + [pl.BlockSpec((CW, width), lambda *at: (0, 0))],
        cam, view_x, kept_view, prob_view, w_full,
        scratch=[pltpu.VMEM((rows, 4 * CW), BF)],
    )
    part, view_out[0] = lax.optimization_barrier((part, view_out[0]))
    chips = tm // 2
    (part,) = call(
        camera_sum_kernel,
        [((chips, width // cams // chips, CW), BF)],
        [VM],
        part,
        scratch=[pltpu.VMEM((width // cams, CW), F32)],
    )
    part = lax.all_to_all(part, "tm", 0, 0, tiled=True, axis_index_groups=same_core)
    view_back = [view_out[0]] + [
        lax.ppermute(view_out[d], "cam", [(i, i ^ d) for i in range(cams)]) for d in range(1, cams)
    ]

    part, near_grad, far_grad, view_back[1:4] = lax.optimization_barrier(
        (part, near_grad, far_grad, view_back[1:4])
    )
    part = jnp.sum(part.astype(F32), axis=0)
    final = width // cams // tm
    mine = lax.dynamic_slice_in_dim(part, core * final, final, 0)
    theirs = lax.ppermute(lax.dynamic_slice_in_dim(part, (1 - core) * final, final, 0), "tm", swap)
    grad_out_weight = jnp.concatenate(
        [jnp.where(core == 0, mine, theirs), jnp.where(core == 0, theirs, mine)], axis=1
    )

    t0, t1 = call(
        time_sum_kernel, [((block, 4 * CW), BF)] * PAIR, [VM] * 5, kept_time, dq_time, own_grad, near_grad, far_grad
    )
    t1 = lax.ppermute(t1, "tm", swap)
    outs = call(
        functools.partial(finish_kernel, cams),
        [((rows, width), BF)] * 4,
        [SM] * 2 + [VM] * (4 + cams),
        me, cam, w_full, action_sum, t0, t1, *view_back,
        scratch=[pltpu.VMEM((rows, 4 * CW), BF)],
    )
    return tuple(a.reshape(1, frames, tokens, width) for a in outs) + (grad_out_weight,)


def solution(mesh):
    in_specs = (
        P("cam", "tm", None, None),
        P("cam", "tm", None, None),
        P("cam", "tm", None, None),
        P("cam", "tm"),
        P(),
        P("tm", None),
        P(),
        P("tm", None),
        P("cam", "tm", None, None),
    )
    out_specs = (
        P("cam", "tm", None, None),
        P("cam", "tm", None, None),
        P("cam", "tm", None, None),
        P("cam", "tm", None, None),
        P(("cam", "tm"), None),
    )
    return jax.shard_map(shards, mesh=mesh, in_specs=in_specs, out_specs=out_specs, check_vma=False)
```
